32 devices in a mesh: grp: 4 (over y, core), mem: 8 (over z, x).
Axes of the slice: x: 2, y: 2, z: 4, core: 2. Of those that a mesh axis runs over, the one named last changes fastest.
Arguments:
- iterate: bfloat16 [4, 2048, 7168], P(None, ('grp', 'mem')), may hold values from -0.5 to 0.5
- slot_of: int32 [4], replicated, may hold values from 0 to 3, each once
Outputs:
- update: bfloat16 [4, 2048, 7168], P(None, ('grp', 'mem'))
The draws below stay inside these ranges and needn't reach their ends.
Inputs may be any that keep to these rules, and one draw needn't show every extreme that they name: `slot_of`: each matrix sits in a different slot.
All inputs are finite; a program needn't handle non-finite values.
Results may differ from the reference program's by a relative error of at most 0.038.
Values may be sent and summed in bfloat16 or wider, within the bound.
No kernel may reach another device: no remote copies, remote signals or barrier semaphores. Data moves between devices by JAX's collectives and lax.ppermute only.
A program may use at most 128 MiB of HBM per device.

```python
import math
import jax
import jax.numpy as jnp
from jax import lax

ROWS = 2048
COLS = 7168
ITERS = 2
MATS = 4
N_MEM = 8


def draw_iterate(key, part):
    key = jax.random.fold_in(key, 11)
    noise_key, column_key, row_key = jax.random.split(key, 3)
    noise = jax.random.truncated_normal(noise_key, -4.0, 4.0, (MATS, ROWS, COLS), jnp.float32)
    trend_power = 1.5
    log_three = math.log(3.0)
    log_ten = math.log(10.0)
    trend_second = (3.0 ** (2.0 * trend_power) - 1.0) / (2.0 * trend_power * log_three)
    trend_fourth = (3.0 ** (4.0 * trend_power) - 1.0) / (4.0 * trend_power * log_three)
    spread_second = 99.0 / (2.0 * log_ten)
    spread_fourth = 9999.0 / (4.0 * log_ten)
    mean_second = trend_second * spread_second
    ratio_value = trend_fourth * spread_fourth / (mean_second * mean_second)
    overall = 0.9 / (math.sqrt(COLS * mean_second) * (1.0 + math.sqrt(ratio_value * ROWS / COLS)))
    position = jnp.arange(COLS, dtype=jnp.float32) / COLS
    column_trend = jnp.exp(trend_power * log_three * position)[None, None, :]
    column_spread = jnp.exp(jax.random.uniform(column_key, (MATS, 1, COLS), jnp.float32, 0.0, log_ten))
    row_scale = jnp.exp(jax.random.uniform(row_key, (MATS, ROWS, 1), jnp.float32, math.log(0.5), 0.0))
    return (noise * row_scale * column_trend * column_spread * overall).astype(jnp.bfloat16)


def setup_inputs(seed: int = 0) -> dict:
    keys = jax.random.split(jax.random.key(seed), 3)
    return {
        "iterate": draw_iterate(jax.random.fold_in(keys[2], 71), 0),
        "slot_of": jax.random.permutation(keys[1], MATS).astype(jnp.int32),
    }


linear_weight = 3.4445
cubic_weight = -4.775
quintic_weight = 2.0315
epsilon = 1e-07

def gram_matrix(current):
    col_width = COLS // N_MEM
    column_blocks = current.reshape(ROWS, N_MEM, col_width).transpose(1, 0, 2)

    def accumulate(running, column_block):
        partial_value = lax.dot_general(column_block, column_block, (((1,), (1,)), ((), ())), preferred_element_type=jnp.float32)
        rounded = lax.optimization_barrier(partial_value.astype(jnp.bfloat16))
        return (running + rounded.astype(jnp.float32), None)
    running, ignored = lax.scan(accumulate, jnp.zeros((ROWS, ROWS), jnp.float32), column_blocks)
    return running.astype(jnp.bfloat16)

def newton_iteration(current):
    gram = gram_matrix(current)
    product = jnp.dot(gram, current, preferred_element_type=jnp.float32).astype(jnp.bfloat16)
    second = jnp.dot(gram, product, preferred_element_type=jnp.float32)
    mixed = linear_weight * current.astype(jnp.float32) + cubic_weight * product.astype(jnp.float32) + quintic_weight * second
    return mixed.astype(jnp.bfloat16)

def reference(iterate, slot_of):
    target = math.sqrt(ROWS * COLS)

    def orthogonalize(slot_index):
        current = lax.dynamic_index_in_dim(iterate, slot_index.astype(jnp.int32), 0, keepdims=False)
        for iteration in range(ITERS):
            current = newton_iteration(current)
        values = current.astype(jnp.float32)
        norm_value = jnp.sqrt(jnp.sum(values * values))
        return (values * (target / (norm_value + epsilon))).astype(jnp.bfloat16)
    return lax.map(orthogonalize, slot_of)
```

```python
import functools
import math

import jax
import jax.numpy as jnp
from jax import lax
from jax.experimental import pallas as pl
from jax.experimental.pallas import tpu as pltpu
from jax.sharding import Mesh, PartitionSpec as P

linear_weight = 3.4445
cubic_weight = -4.775
quintic_weight = 2.0315
epsilon = 1e-07

every = ("grp", "plane", "sub")
team = ("grp", "sub")
MIB = 1024 * 1024


def dot(a, b):
    return jnp.dot(a, b, preferred_element_type=jnp.float32)


def dot_t(a, b):
    return lax.dot_general(a, b, (((1,), (1,)), ((), ())), preferred_element_type=jnp.float32)


def params(mib):
    return pltpu.CompilerParams(vmem_limit_bytes=mib * MIB)


def device_index():
    planes = lax.axis_size("plane")
    sub = lax.axis_size("sub")
    return (lax.axis_index("grp") * planes + lax.axis_index("plane")) * sub + lax.axis_index("sub")


def member_index():
    return lax.axis_index("grp") * lax.axis_size("sub") + lax.axis_index("sub")


def in_hbm(value):
    return pltpu.with_memory_space_constraint(value, pltpu.HBM)


def in_vmem(value):
    return pltpu.with_memory_space_constraint(value, pltpu.VMEM)


HBM = pl.BlockSpec(memory_space=pltpu.HBM)
ONCHIP = pl.BlockSpec(memory_space=pltpu.VMEM)


def pack_kernel(slot_ref, x_ref, o_ref, held, load_sems, store_sems):
    outer, mats, sub, _, width = o_ref.shape
    loads = [
        pltpu.make_async_copy(x_ref.at[slot_ref[m]], held.at[m], load_sems.at[m])
        for m in range(mats)
    ]
    for load in loads[:2]:
        load.start()
    stores = []
    for m in range(mats):
        loads[m].wait()
        if m + 2 < mats:
            loads[m + 2].start()
        for g in range(outer):
            for s in range(sub):
                at = (g * sub + s) * width
                store = pltpu.make_async_copy(
                    held.at[m, :, at : at + width], o_ref.at[g, m, s], store_sems.at[len(stores)]
                )
                store.start()
                stores.append(store)
    for store in stores:
        store.wait()


def pack(iterate, slot_of, outer, sub):
    mats, rows, cols = iterate.shape
    width = cols // (outer * sub)
    return pl.pallas_call(
        pack_kernel,
        grid_spec=pltpu.PrefetchScalarGridSpec(
            num_scalar_prefetch=1,
            grid=(1,),
            in_specs=[HBM],
            out_specs=HBM,
            scratch_shapes=[
                pltpu.VMEM(iterate.shape, iterate.dtype),
                pltpu.SemaphoreType.DMA((mats,)),
                pltpu.SemaphoreType.DMA((mats * outer * sub,)),
            ],
        ),
        out_shape=pltpu.HBM((outer, mats, sub, rows, width), iterate.dtype),
        compiler_params=params(8),
        cost_estimate=pl.CostEstimate(
            flops=0, bytes_accessed=4 * iterate.size, transcendentals=0
        ),
        name="pack",
    )(in_hbm(slot_of), in_hbm(iterate))


def head_rows(width):
    return width // 2 + width // 4


def packed_rows(rows, width):
    return head_rows(width) + (rows // 2 - width) + width // 2


def write_head(o_ref, block):
    half, quarter = block.shape[0] // 2, block.shape[0] // 4
    o_ref[:half] = block[:half]
    o_ref[half : half + quarter, :half] = block[half : half + quarter, half:]
    o_ref[half : half + quarter, half:] = block[half + quarter :, half:]


def gram_strip(x_ref, d, o_ref):
    rows, _ = x_ref.shape
    blocks = lax.axis_size(team)
    width = rows // blocks
    half = blocks // 2
    head = head_rows(width)
    tail = head + (half - 1) * width
    for i in range(blocks):

        @pl.when(d == i)
        def _(i=i):
            mine = x_ref[i * width : (i + 1) * width].T
            first = min(half, blocks - i)
            value = dot(x_ref[i * width : (i + first) * width], mine).astype(o_ref.dtype)
            write_head(o_ref, value[:width])
            split = head + (first - 1) * width
            if first > 1:
                o_ref[head:split] = value[width:]
            if first < half:
                o_ref[split:tail] = dot(x_ref[: (half - first) * width], mine).astype(o_ref.dtype)
            if i < half:
                at = (i + half) * width
                last = dot(x_ref[at : at + width // 2], mine)
            else:
                at = (i - half) * width
                last = dot_t(
                    x_ref[i * width + width // 2 : (i + 1) * width], x_ref[at : at + width]
                )
            o_ref[tail:] = last.astype(o_ref.dtype)


def gram_strips(x_ref, o_ref, masks):
    index = member_index()

    @pl.loop(0, len(masks))
    def _(k):
        mask = masks[0]
        for i, value in enumerate(masks):
            mask = jnp.where(k == i, value, mask)
        gram_strip(x_ref, index ^ mask, o_ref.at[k])


def gram_kernel(masks, x_ref, o_ref):
    gram_strips(x_ref, o_ref, masks)


def gram(current, masks):
    rows, cols = current.shape
    count = len(masks)
    width = rows // lax.axis_size(team)
    packed = packed_rows(rows, width)
    return pl.pallas_call(
        functools.partial(gram_kernel, masks),
        in_specs=[ONCHIP],
        out_specs=ONCHIP,
        out_shape=pltpu.VMEM((count, packed, width), current.dtype),
        compiler_params=params(16),
        cost_estimate=pl.CostEstimate(
            flops=2 * count * packed * width * cols,
            bytes_accessed=2 * (current.size + count * packed * width),
            transcendentals=0,
        ),
        name="gram",
    )(in_vmem(current))


def add(a, b):
    return (a.astype(jnp.float32) + b.astype(jnp.float32)).astype(a.dtype)


def swap(value, mask):
    pairs = [(i, i ^ mask) for i in range(lax.axis_size(team))]
    return lax.ppermute(value, team, pairs)


def masks(sub):
    along_x, core, along_y = 1, sub, 2 * sub
    near = [0, along_x, along_y, along_x + along_y]
    return near + [core + mask for mask in near]


def scatter_sum(current, sub):
    along_x, core, along_y = 1, sub, 2 * sub
    arrived = swap(gram(current, masks(sub)[4:]), core)
    total = add(gram(current, masks(sub)[:4]), arrived)
    cut = total.shape[1] // 2
    upper, lower = total[:, :cut], total[:, cut:]
    from_x = swap(upper[1::2], along_x)
    from_y = swap(lower[2:], along_y)
    upper = add(upper[::2], from_x)
    lower = add(lower[:2], from_y)
    from_y = swap(upper[1], along_y)
    from_x = swap(lower[1], along_x)
    return add(upper[0], from_y), add(lower[0], from_x)


def gather_first(upper, lower, sub):
    along_x, core, along_y = 1, sub, 2 * sub
    lower_x = swap(lower, along_x)
    upper_y = swap(upper, along_y)
    lower_core = swap(lower, core)
    late, lower_core = lax.optimization_barrier(((upper, lower), lower_core))
    upper_x = swap(late[0], along_x)
    lower_y = swap(late[1], along_y)
    upper_xy = swap(upper_y, along_x)
    lower_xy = swap(lower_x, along_y)
    here = [upper, lower, upper_x, lower_x, upper_y, lower_y, upper_xy, lower_xy]
    return here + [swap(upper, core), lower_core] + [swap(value, core) for value in here[2:]]


def gather_second(upper, lower, strip, sub, first_work, second_work):
    along_x, core, along_y = 1, sub, 2 * sub
    dtype = strip.dtype
    lower_x = swap(lower, along_x)
    upper_y = swap(upper, along_y)
    upper_x = swap(upper, along_x)
    lower_y = swap(lower, along_y)
    other = swap(strip, core)
    result = first_work()
    lower_x, upper_y, result = lax.optimization_barrier((lower_x, upper_y, result))
    far = swap(upper_y, along_x), swap(lower_x, along_y)
    result = second_work(result)
    x = jnp.concatenate([upper_x, lower_x])
    y = jnp.concatenate([upper_y, lower_y])
    parts = [strip, other, x, y, swap(x, core), swap(y, core)]
    places = [0, core, along_x, along_y, core + along_x, core + along_y]
    far, result = lax.optimization_barrier((far, result))
    last = [swap(half, core) for half in far]
    full = spread(parts, places, dtype)
    last, full = lax.optimization_barrier((last, full))
    return full, [*far, *last], result


def block_of(index, width):
    return pl.ds(pl.multiple_of(index * width, width), width)


def fill_strip(full, strip, d, blocks, width):
    half = blocks // 2
    head = head_rows(width)
    tail = head + (half - 1) * width
    middle, quarter = width // 2, width // 4
    column = block_of(d, width)
    lower = pl.ds(pl.multiple_of(d * width + middle, middle), middle)
    full[pl.ds(pl.multiple_of(d * width, width), middle), column] = strip[:middle]
    full[lower, pl.ds(pl.multiple_of(d * width, width), middle)] = strip[:middle, middle:].T
    for i in range(2):
        at = pl.ds(pl.multiple_of(d * width + middle + i * quarter, quarter), quarter)
        full[at, lower] = strip[middle : middle + quarter, i * middle : (i + 1) * middle]
    across = strip[head:tail].T
    for k in range(1, half):
        r = block_of(lax.rem(d + k, blocks), width)
        full[r, column] = strip[head + (k - 1) * width : head + k * width]
        full[column, r] = across[:, (k - 1) * width : k * width]
    low = d < half
    c = block_of(jnp.where(low, d, d - half), width)
    start = jnp.where(low, (d + half) * width, d * width + middle)
    r = pl.ds(pl.multiple_of(start, middle), middle)
    piece = strip[tail:]
    full[r, c] = piece
    full[c, r] = piece.T


def spread_kernel(places, *refs):
    full = refs[-1]
    blocks = lax.axis_size(team)
    width = full.shape[0] // blocks
    for i, mask in enumerate(places):
        fill_strip(full, refs[i], member_index() ^ mask, blocks, width)


def spread(strips, places, dtype):
    height, width = strips[0].shape
    rows = width * lax.axis_size(team)
    return pl.pallas_call(
        functools.partial(spread_kernel, places),
        in_specs=[ONCHIP] * len(strips),
        out_specs=ONCHIP,
        out_shape=pltpu.VMEM((rows, rows), dtype),
        compiler_params=params(16),
        cost_estimate=pl.CostEstimate(
            flops=height * width * 256 * len(strips),
            bytes_accessed=6 * len(strips) * height * width,
            transcendentals=0,
        ),
        name="spread",
    )(*[in_vmem(strip) for strip in strips])


def fill_halves(full, halves, places, strip):
    blocks = lax.axis_size(team)
    width = full.shape[0] // blocks
    cut = strip.shape[0] // 2
    for i, mask in enumerate(places):
        strip[:cut] = halves[2 * i][...]
        strip[cut:] = halves[2 * i + 1][...]
        fill_strip(full, strip, member_index() ^ mask, blocks, width)


def polynomial_kernel(chunk, *refs):
    halves = refs[:-7]
    full, upper_out, lower_out, out, poly, middle, last = refs[-7:]
    rows = full.shape[0]
    packed, width = out.shape
    blocks = rows // width
    half = blocks // 2
    fill_halves(full, halves, masks(lax.axis_size("sub")), out)
    index = member_index()
    mine = block_of(index, width)

    @pl.loop(0, rows // chunk)
    def _(r):
        at = block_of(r, chunk)
        value = cubic_weight * full[at, mine].astype(jnp.float32) + quintic_weight * dot(
            full[at, :], full[:, mine]
        )
        row = lax.broadcasted_iota(jnp.int32, value.shape, 0) + r * chunk
        col = lax.broadcasted_iota(jnp.int32, value.shape, 1) + index * width
        value = value + jnp.where(row == col, linear_weight, 0.0)
        poly[at, :] = value.astype(poly.dtype)

    @pl.loop(0, rows // chunk)
    def _(r):
        at = block_of(r, chunk)
        middle[at, :] = dot(full[at, :], poly[...]).astype(middle.dtype)

    @pl.loop(0, rows // chunk)
    def _(r):
        at = block_of(r, chunk)
        poly[at, :] = (
            cubic_weight * middle[at, :].astype(jnp.float32)
            + quintic_weight * dot(full[at, :], middle[...])
        ).astype(poly.dtype)

    pair = 2 * width

    @pl.loop(0, blocks // 4 + 1)
    def _(j):
        at = block_of(lax.rem(lax.div(index, 2) + j, blocks // 2), pair)
        value = linear_weight * middle[at, :].astype(jnp.float32)
        last[at, :] = (value + dot(full[at, :], poly[...])).astype(last.dtype)

    head = head_rows(width)
    tail = head + (half - 1) * width
    write_head(out, last[mine, :])
    for k in range(1, half):
        at = block_of(lax.rem(index + k, blocks), width)
        out[head + (k - 1) * width : head + k * width] = last[at, :]
    other = pl.multiple_of(lax.rem(index + half, blocks) * width, width)

    @pl.when(index < half)
    def _():
        out[tail:] = last[pl.ds(other, width // 2), :]

    @pl.when(index >= half)
    def _():
        out[tail:] = last[pl.ds(other, width), width // 2 :].T

    upper_out[...] = out[: packed // 2]
    lower_out[...] = out[packed // 2 :]


def polynomial(halves):
    cut, width = halves[0].shape
    rows = width * len(halves) // 2
    dtype = halves[0].dtype
    return pl.pallas_call(
        functools.partial(polynomial_kernel, 1024),
        in_specs=[ONCHIP] * len(halves),
        out_specs=[ONCHIP] * 4,
        out_shape=[
            pltpu.VMEM((rows, rows), dtype),
            pltpu.VMEM((cut, width), dtype),
            pltpu.VMEM((cut, width), dtype),
            pltpu.VMEM((2 * cut, width), dtype),
        ],
        scratch_shapes=[pltpu.VMEM((rows, width), dtype)] * 3,
        compiler_params=params(16),
        cost_estimate=pl.CostEstimate(
            flops=8 * rows * rows * width, bytes_accessed=4 * rows * rows, transcendentals=0
        ),
        name="polynomial",
    )(*[in_vmem(half) for half in halves])


def columns(cols, first=0):
    return [slice(c, min(c + 256, cols)) for c in range(first, cols, 256)]


LATE = 256


def product_kernel(
    chunk, gram_ref, x_ref, o_ref, gram_out, late_out, late_product_out, late_product, sems
):
    rows, cols = o_ref.shape
    stores = [
        pltpu.make_async_copy(gram_ref, gram_out, sems.at[0]),
        pltpu.make_async_copy(x_ref.at[:, cols:], late_out, sems.at[1]),
    ]
    for store in stores:
        store.start()

    @pl.loop(0, rows // chunk)
    def _(r):
        at = block_of(r, chunk)
        late_product[at, :] = dot(gram_ref[at, :], x_ref[:, cols:]).astype(o_ref.dtype)

    stores.append(pltpu.make_async_copy(late_product, late_product_out, sems.at[2]))
    stores[2].start()

    @pl.loop(0, rows // chunk)
    def _(r):
        at = block_of(r, chunk)
        for c in columns(cols):
            o_ref[at, c] = dot(gram_ref[at, :], x_ref[:, c]).astype(o_ref.dtype)

    for store in stores:
        store.wait()


def step_start(gram_whole, current):
    rows, cols = current.shape
    dtype = current.dtype
    return pl.pallas_call(
        functools.partial(product_kernel, 1024),
        in_specs=[ONCHIP] * 2,
        out_specs=[ONCHIP, HBM, HBM, HBM],
        out_shape=[
            pltpu.VMEM((rows, cols - LATE), dtype),
            pltpu.HBM((rows, rows), dtype),
            pltpu.HBM((rows, LATE), dtype),
            pltpu.HBM((rows, LATE), dtype),
        ],
        scratch_shapes=[pltpu.VMEM((rows, LATE), dtype), pltpu.SemaphoreType.DMA((3,))],
        compiler_params=params(16),
        cost_estimate=pl.CostEstimate(
            flops=2 * rows * rows * cols, bytes_accessed=4 * rows * rows, transcendentals=0
        ),
        name="product",
    )(in_vmem(gram_whole), in_vmem(current))


def mix_kernel(chunk, gram_ref, x_ref, product_ref, o_ref):
    rows, cols = o_ref.shape

    @pl.loop(0, rows // chunk)
    def _(r):
        at = block_of(r, chunk)
        for c in columns(cols):
            second = dot(gram_ref[at, :], product_ref[:, c])
            o_ref[at, c] = mix(x_ref[at, c], product_ref[at, c], second)


def step_end(gram_whole, current, product):
    rows, cols = product.shape
    return pl.pallas_call(
        functools.partial(mix_kernel, 1024),
        in_specs=[ONCHIP] * 3,
        out_specs=ONCHIP,
        out_shape=pltpu.VMEM((rows, cols), current.dtype),
        compiler_params=params(16),
        cost_estimate=pl.CostEstimate(
            flops=2 * rows * rows * cols, bytes_accessed=2 * rows * rows, transcendentals=0
        ),
        name="mix",
    )(in_vmem(gram_whole), in_vmem(current), in_vmem(product))


SUM_ROWS = 16


def write_pieces(o_ref, value, r, chunk, local_rows, tile):
    cols = value.shape[1]
    per = chunk // local_rows
    for p in range(per):
        for t in range(cols // 128):
            o_ref[r * per + p, (tile + t) * local_rows : (tile + t + 1) * local_rows, :] = value[
                p * local_rows : (p + 1) * local_rows, t * 128 : (t + 1) * 128
            ]


def mix(current, product, second):
    return (
        linear_weight * current.astype(jnp.float32)
        + cubic_weight * product.astype(jnp.float32)
        + quintic_weight * second
    ).astype(current.dtype)


def first_part_kernel(local_rows, chunk, *refs):
    halves, x_ref = refs[:4], refs[5]
    full, gram_out, rest_out, o_ref, sum_ref, strip, product, pieces, sems = refs[6:]
    rows, cols = product.shape
    store_rest = pltpu.make_async_copy(x_ref.at[:, cols:], rest_out, sems.at[0])
    store_rest.start()
    fill_halves(full, halves, masks(lax.axis_size("sub"))[3::4], strip)
    store_gram = pltpu.make_async_copy(full, gram_out, sems.at[1])
    store_gram.start()
    sum_ref[...] = jnp.zeros_like(sum_ref)

    def stores(r):
        at = block_of(r, chunk // local_rows)
        return pltpu.make_async_copy(pieces.at[at], o_ref.at[at], sems.at[2 + r])

    @pl.loop(0, rows // chunk)
    def _(r):
        at = block_of(r, chunk)
        product[at, :] = dot(full[at, :], x_ref[:, :cols]).astype(product.dtype)

    @pl.loop(0, rows // chunk)
    def _(r):
        at = block_of(r, chunk)
        mixed = mix(x_ref[at, :cols], product[at, :], dot(full[at, :], product[...]))
        write_pieces(pieces, mixed, r, chunk, local_rows, 0)
        stores(r).start()
        value = mixed.astype(jnp.float32)
        sum_ref[...] += jnp.sum(value * value, axis=0, keepdims=True)

    store_rest.wait()
    store_gram.wait()
    for r in range(rows // chunk):
        stores(r).wait()


def first_part(full, halves, current, cols, local_rows):
    cut, width = halves[0].shape
    rows, col_count = current.shape
    dtype = current.dtype
    shape = (rows // local_rows, cols // 128 * local_rows, 128)
    return pl.pallas_call(
        functools.partial(first_part_kernel, local_rows, 1024),
        in_specs=[ONCHIP] * 6,
        out_specs=[ONCHIP, HBM, HBM, HBM, ONCHIP],
        out_shape=[
            pltpu.VMEM((rows, rows), dtype),
            pltpu.HBM((rows, rows), dtype),
            pltpu.HBM((rows, col_count - cols), dtype),
            pltpu.HBM(shape, dtype),
            pltpu.VMEM((1, cols), jnp.float32),
        ],
        input_output_aliases={4: 0},
        scratch_shapes=[
            pltpu.VMEM((2 * cut, width), dtype),
            pltpu.VMEM((rows, cols), dtype),
            pltpu.VMEM(shape, dtype),
            pltpu.SemaphoreType.DMA((2 + rows // 1024,)),
        ],
        compiler_params=params(16),
        cost_estimate=pl.CostEstimate(
            flops=4 * rows * rows * cols, bytes_accessed=4 * rows * rows, transcendentals=0
        ),
        name="first_part",
    )(*[in_vmem(half) for half in halves], in_vmem(full), in_vmem(current))[1:]


def sum_rows(total, dtype):
    high = total.astype(dtype)
    rest = jnp.where(total < jnp.inf, total - high.astype(jnp.float32), 0.0)
    middle = rest.astype(dtype)
    low = rest - middle.astype(jnp.float32)
    row = lax.broadcasted_iota(jnp.int32, (SUM_ROWS, 128), 0)
    parts = jnp.where(row == 0, high.astype(jnp.float32), 0.0)
    parts = jnp.where(row == 1, middle.astype(jnp.float32), parts)
    return jnp.where(row == 2, low, parts).astype(dtype)


def second_part_kernel(
    local_rows,
    chunk,
    before_hbm,
    late_hbm,
    late_product_hbm,
    gram_hbm,
    x_hbm,
    sum_ref,
    o_ref,
    before,
    full,
    late,
    late_product,
    x,
    product,
    total,
    pieces,
    sems,
    block_sems,
):
    rows, cols = x.shape
    count = rows // chunk
    early = cols - late.shape[1]
    body = cols // 128 * local_rows
    load_late = pltpu.make_async_copy(late_hbm, late, sems.at[0])
    load_product = pltpu.make_async_copy(late_product_hbm, late_product, sems.at[1])
    load_x = pltpu.make_async_copy(x_hbm, x.at[:, :early], sems.at[2])

    def loads(k, r):
        source, target = ((before_hbm, before), (gram_hbm, full))[k]
        at = block_of(r, chunk)
        return pltpu.make_async_copy(source.at[at, :], target.at[at, :], block_sems.at[k, r])

    def stores(r):
        at = block_of(r, chunk // local_rows)
        return pltpu.make_async_copy(
            pieces.at[at, :body, :], o_ref.at[at, :body, :], block_sems.at[2, r]
        )

    load_product.start()
    loads(0, 0).start()
    load_late.start()
    load_product.wait()
    load_late.wait()
    load_x.start()

    @pl.loop(0, count)
    def _(r):
        loads(0, r).wait()

        @pl.when(r + 1 < count)
        def _():
            loads(0, r + 1).start()

        @pl.when(r + 1 == count)
        def _():
            loads(1, 0).start()

        at = block_of(r, chunk)
        second = dot(before[at, :], late_product[...])
        x[at, early:] = mix(late[at, :], late_product[at, :], second)

    load_x.wait()

    @pl.loop(0, count)
    def _(r):
        loads(1, r).wait()

        @pl.when(r + 1 < count)
        def _():
            loads(1, r + 1).start()

        at = block_of(r, chunk)
        for c in columns(cols):
            product[at, c] = dot(full[at, :], x[:, c]).astype(product.dtype)

    total[...] = jnp.zeros_like(total)

    @pl.loop(0, count)
    def _(r):
        at = block_of(r, chunk)
        for c in columns(cols):
            mixed = mix(x[at, c], product[at, c], dot(full[at, :], product[:, c]))
            write_pieces(pieces, mixed, r, chunk, local_rows, c.start // 128)
            value = mixed.astype(jnp.float32)
            total[:, c] += jnp.sum(value * value, axis=0, keepdims=True)
        stores(r).start()

    tail = sum_rows(
        jnp.sum(total[...], axis=1, keepdims=True)
        + jnp.sum(sum_ref[...], axis=1, keepdims=True),
        o_ref.dtype,
    )
    for p in range(o_ref.shape[0]):
        pieces[p, body:, :] = tail
    store = pltpu.make_async_copy(pieces.at[:, body:, :], o_ref.at[:, body:, :], sems.at[3])
    store.start()
    for r in range(count):
        stores(r).wait()
    store.wait()


def second_part(before, late, late_product, gram_whole, current, sums, local_rows):
    rows, early = current.shape
    cols = early + late.shape[1]
    dtype = current.dtype
    chunk = 512
    shape = (rows // local_rows, cols // 128 * local_rows + SUM_ROWS, 128)
    return pl.pallas_call(
        functools.partial(second_part_kernel, local_rows, chunk),
        in_specs=[HBM] * 5 + [ONCHIP],
        out_specs=HBM,
        out_shape=pltpu.HBM(shape, dtype),
        scratch_shapes=[
            pltpu.VMEM((rows, rows), dtype),
            pltpu.VMEM((rows, rows), dtype),
            pltpu.VMEM(late.shape, dtype),
            pltpu.VMEM(late.shape, dtype),
            pltpu.VMEM((rows, cols), dtype),
            pltpu.VMEM((rows, cols), dtype),
            pltpu.VMEM((1, cols), jnp.float32),
            pltpu.VMEM(shape, dtype),
            pltpu.SemaphoreType.DMA((4,)),
            pltpu.SemaphoreType.DMA((3, rows // chunk)),
        ],
        compiler_params=params(40),
        cost_estimate=pl.CostEstimate(
            flops=4 * rows * rows * (cols + late.shape[1]),
            bytes_accessed=8 * rows * rows,
            transcendentals=0,
        ),
        name="second_part",
    )(
        *[in_hbm(value) for value in (before, late, late_product, gram_whole, current)],
        in_vmem(sums),
    )


def scaled_kernel(target, first_ref, second_ref, o_ref):
    outer, _, sub, _, _ = first_ref.shape
    local_rows = o_ref.shape[1]
    tiles = first_ref.shape[3] // local_rows
    more = second_ref.shape[3] // local_rows
    total = jnp.zeros((1, 128), jnp.float32)
    for g in range(outer):
        for s in range(sub):
            parts = second_ref[g, 0, s, more * local_rows :, :].astype(jnp.float32)
            total = total + jnp.sum(parts, axis=0, keepdims=True)
    scale = target / (jnp.sqrt(total) + epsilon)
    at = 0
    for g in range(outer):
        for s in range(sub):
            for t in range(tiles + more):
                if t < tiles:
                    value = first_ref[g, 0, s, t * local_rows : (t + 1) * local_rows, :]
                else:
                    u = t - tiles
                    value = second_ref[g, 0, s, u * local_rows : (u + 1) * local_rows, :]
                o_ref[0, :, at : at + 128] = (value.astype(jnp.float32) * scale).astype(
                    o_ref.dtype
                )
                at += 128


def scaled(first, second, local_rows, target):
    outer, mats, sub, height, _ = first.shape
    height_more = second.shape[3]
    cols = outer * sub * 128 * (height // local_rows + height_more // local_rows)
    return pl.pallas_call(
        functools.partial(scaled_kernel, target),
        grid=(mats,),
        in_specs=[
            pl.BlockSpec((outer, 1, sub, height, 128), lambda m: (0, m, 0, 0, 0)),
            pl.BlockSpec((outer, 1, sub, height_more, 128), lambda m: (0, m, 0, 0, 0)),
        ],
        out_specs=pl.BlockSpec((1, local_rows, cols), lambda m: (m, 0, 0)),
        out_shape=jax.ShapeDtypeStruct((mats, local_rows, cols), first.dtype),
        compiler_params=params(14),
        cost_estimate=pl.CostEstimate(
            flops=first.size + second.size,
            bytes_accessed=4 * (first.size + second.size),
            transcendentals=0,
        ),
        name="scaled",
    )(first, second)


def plain_strip(gram, index, width):
    strip = lax.dynamic_slice_in_dim(gram, index * width, width, axis=1)
    row = lax.broadcasted_iota(jnp.int32, strip.shape, 0)
    col = lax.broadcasted_iota(jnp.int32, strip.shape, 1) + index * width
    poly = (
        jnp.where(row == col, linear_weight, 0.0)
        + cubic_weight * strip.astype(jnp.float32)
        + quintic_weight * dot(gram, strip)
    ).astype(jnp.bfloat16)
    middle = dot(gram, poly).astype(jnp.bfloat16)
    middle_f = middle.astype(jnp.float32)
    inner = (cubic_weight * middle_f + quintic_weight * dot(gram, middle)).astype(jnp.bfloat16)
    return (linear_weight * middle_f + dot(gram, inner)).astype(jnp.bfloat16)


def plain_step(gram, current):
    product = dot(gram, current).astype(jnp.bfloat16)
    return mix(current, product, dot(gram, product))


def exchange(pieces):
    return lax.all_to_all(pieces, every, split_axis=0, concat_axis=0, tiled=True)


def kernel_path(iterate, slot_of, outer, groups, sub):
    members = outer * sub
    mats, local_rows, col_count = iterate.shape
    col_width = col_count // members
    rows = local_rows * groups * members
    pieces = pack(iterate, slot_of, outer, sub)
    arrived = exchange(pieces.reshape(mats * members, local_rows, col_width))
    current = arrived.reshape(rows, col_width)
    gram_whole, upper, lower, strip = polynomial(gather_first(*scatter_sum(current, sub), sub))

    def first_work():
        return step_start(gram_whole, current)

    def second_work(done):
        product, *kept = done
        return step_end(gram_whole, current, product), kept

    full, halves, (stepped, kept) = gather_second(
        upper, lower, strip, sub, first_work, second_work
    )
    whole, rest, first, sums = first_part(full, halves, stepped, 256, local_rows)
    first = exchange(first)
    second = exchange(second_part(*kept, whole, rest, sums, local_rows))
    return scaled(
        first.reshape(outer, mats, sub, -1, 128),
        second.reshape(outer, mats, sub, -1, 128),
        local_rows,
        math.sqrt(rows * col_count),
    )


def plain_path(iterate, slot_of, outer, groups, sub):
    members = outer * sub
    mats, local_rows, col_count = iterate.shape
    col_width = col_count // members
    rows = local_rows * groups * members
    pieces = jnp.take(iterate, slot_of, axis=0)
    pieces = pieces.reshape(mats, local_rows, outer, sub, col_width).transpose(2, 0, 3, 1, 4)
    arrived = exchange(pieces.reshape(mats * members, local_rows, col_width))
    current = arrived.reshape(rows, col_width)
    partial = dot_t(current, current).astype(jnp.bfloat16)
    owned = lax.psum_scatter(partial, team, scatter_dimension=0, tiled=True)
    gram = lax.all_gather(owned, team, axis=0, tiled=True)
    strip = plain_strip(gram, lax.axis_index(team), rows // members)
    gram_next = lax.all_gather(strip.T, team, axis=0, tiled=True)
    current = plain_step(gram, current)
    current = plain_step(gram_next, current)
    values = current.astype(jnp.float32)
    sum_total = lax.psum(jnp.sum(values * values), team)
    scale = math.sqrt(rows * col_count) / (jnp.sqrt(sum_total) + epsilon)
    leaving = (values * scale).astype(jnp.bfloat16)
    returned = exchange(leaving.reshape(groups * members, local_rows, col_width))
    returned = returned.reshape(outer, mats, sub, local_rows, col_width)
    return returned.transpose(1, 3, 0, 2, 4).reshape(mats, local_rows, col_count)


def on_device(iterate, slot_of):
    groups = lax.axis_size("plane")
    sub = lax.axis_size("sub")
    outer = lax.axis_size("grp")
    members = outer * sub
    _, local_rows, col_count = iterate.shape
    col_width = col_count // members
    strip_width = local_rows * groups
    fits = (
        col_width % 128 == 0
        and col_width > 256 + LATE
        and strip_width % 256 == 0
        and local_rows % 16 == 0
        and sub == 2
        and outer == 4
        and groups == 4
    )
    return (kernel_path if fits else plain_path)(iterate, slot_of, outer, groups, sub)


def solution(mesh):
    outer, inner = mesh.devices.shape
    split = Mesh(mesh.devices.reshape(outer, outer, inner // outer), every)
    spec = P(None, every, None)
    return jax.shard_map(
        on_device,
        mesh=split,
        in_specs=(spec, P()),
        out_specs=spec,
        check_vma=False,
    )
```

```python
import functools
import math

import jax
import jax.numpy as jnp
from jax import lax
from jax.experimental import pallas as pl
from jax.experimental.pallas import tpu as pltpu
from jax.sharding import Mesh, PartitionSpec as P

linear_weight = 3.4445
cubic_weight = -4.775
quintic_weight = 2.0315
epsilon = 1e-07

every = ("grp", "plane", "sub")
team = ("grp", "sub")
MIB = 1024 * 1024


def dot(a, b):
    return jnp.dot(a, b, preferred_element_type=jnp.float32)


def dot_t(a, b):
    return lax.dot_general(a, b, (((1,), (1,)), ((), ())), preferred_element_type=jnp.float32)


def params(mib):
    return pltpu.CompilerParams(vmem_limit_bytes=mib * MIB)


def device_index():
    planes = lax.axis_size("plane")
    sub = lax.axis_size("sub")
    return (lax.axis_index("grp") * planes + lax.axis_index("plane")) * sub + lax.axis_index("sub")


def member_index():
    return lax.axis_index("grp") * lax.axis_size("sub") + lax.axis_index("sub")


def in_hbm(value):
    return pltpu.with_memory_space_constraint(value, pltpu.HBM)


def in_vmem(value):
    return pltpu.with_memory_space_constraint(value, pltpu.VMEM)


HBM = pl.BlockSpec(memory_space=pltpu.HBM)
ONCHIP = pl.BlockSpec(memory_space=pltpu.VMEM)


def pack_kernel(slot_ref, x_ref, o_ref, held, load_sems, store_sems):
    outer, mats, sub, _, width = o_ref.shape
    loads = [
        pltpu.make_async_copy(x_ref.at[slot_ref[m]], held.at[m], load_sems.at[m])
        for m in range(mats)
    ]
    for load in loads:
        load.start()
    stores = []
    for m in range(mats):
        loads[m].wait()
        for g in range(outer):
            for s in range(sub):
                at = (g * sub + s) * width
                store = pltpu.make_async_copy(
                    held.at[m, :, at : at + width], o_ref.at[g, m, s], store_sems.at[len(stores)]
                )
                store.start()
                stores.append(store)
    for store in stores:
        store.wait()


def pack(iterate, slot_of, outer, sub):
    mats, rows, cols = iterate.shape
    width = cols // (outer * sub)
    return pl.pallas_call(
        pack_kernel,
        grid_spec=pltpu.PrefetchScalarGridSpec(
            num_scalar_prefetch=1,
            grid=(1,),
            in_specs=[HBM],
            out_specs=HBM,
            scratch_shapes=[
                pltpu.VMEM(iterate.shape, iterate.dtype),
                pltpu.SemaphoreType.DMA((mats,)),
                pltpu.SemaphoreType.DMA((mats * outer * sub,)),
            ],
        ),
        out_shape=pltpu.HBM((outer, mats, sub, rows, width), iterate.dtype),
        compiler_params=params(8),
        cost_estimate=pl.CostEstimate(
            flops=0, bytes_accessed=4 * iterate.size, transcendentals=0
        ),
        name="pack",
    )(in_hbm(slot_of), in_hbm(iterate))


def head_rows(width):
    return width // 2 + width // 4


def packed_rows(rows, width):
    return head_rows(width) + (rows // 2 - width) + width // 2


def write_head(o_ref, block):
    half, quarter = block.shape[0] // 2, block.shape[0] // 4
    o_ref[:half] = block[:half]
    o_ref[half : half + quarter, :half] = block[half : half + quarter, half:]
    o_ref[half : half + quarter, half:] = block[half + quarter :, half:]


def gram_strip(x_ref, d, o_ref):
    rows, _ = x_ref.shape
    blocks = lax.axis_size(team)
    width = rows // blocks
    half = blocks // 2
    head = head_rows(width)
    tail = head + (half - 1) * width
    for i in range(blocks):

        @pl.when(d == i)
        def _(i=i):
            mine = x_ref[i * width : (i + 1) * width].T
            first = min(half, blocks - i)
            value = dot(x_ref[i * width : (i + first) * width], mine).astype(o_ref.dtype)
            write_head(o_ref, value[:width])
            split = head + (first - 1) * width
            if first > 1:
                o_ref[head:split] = value[width:]
            if first < half:
                o_ref[split:tail] = dot(x_ref[: (half - first) * width], mine).astype(o_ref.dtype)
            if i < half:
                at = (i + half) * width
                last = dot(x_ref[at : at + width // 2], mine)
            else:
                at = (i - half) * width
                last = dot_t(
                    x_ref[i * width + width // 2 : (i + 1) * width], x_ref[at : at + width]
                )
            o_ref[tail:] = last.astype(o_ref.dtype)


def gram_strips(x_ref, o_ref, masks):
    index = member_index()

    @pl.loop(0, len(masks))
    def _(k):
        mask = masks[0]
        for i, value in enumerate(masks):
            mask = jnp.where(k == i, value, mask)
        gram_strip(x_ref, index ^ mask, o_ref.at[k])


def gram_kernel(masks, x_ref, o_ref):
    gram_strips(x_ref, o_ref, masks)


def gram(current, masks):
    rows, cols = current.shape
    count = len(masks)
    width = rows // lax.axis_size(team)
    packed = packed_rows(rows, width)
    return pl.pallas_call(
        functools.partial(gram_kernel, masks),
        in_specs=[ONCHIP],
        out_specs=ONCHIP,
        out_shape=pltpu.VMEM((count, packed, width), current.dtype),
        compiler_params=params(16),
        cost_estimate=pl.CostEstimate(
            flops=2 * count * packed * width * cols,
            bytes_accessed=2 * (current.size + count * packed * width),
            transcendentals=0,
        ),
        name="gram",
    )(in_vmem(current))


def add(a, b):
    return (a.astype(jnp.float32) + b.astype(jnp.float32)).astype(a.dtype)


def swap(value, mask):
    pairs = [(i, i ^ mask) for i in range(lax.axis_size(team))]
    return lax.ppermute(value, team, pairs)


def masks(sub):
    along_x, core, along_y = 1, sub, 2 * sub
    near = [0, along_x, along_y, along_x + along_y]
    return near + [core + mask for mask in near]


def scatter_sum(current, sub):
    along_x, core, along_y = 1, sub, 2 * sub
    arrived = swap(gram(current, masks(sub)[4:]), core)
    total = add(gram(current, masks(sub)[:4]), arrived)
    cut = total.shape[1] // 2
    upper, lower = total[:, :cut], total[:, cut:]
    from_x = swap(upper[1::2], along_x)
    from_y = swap(lower[2:], along_y)
    upper = add(upper[::2], from_x)
    lower = add(lower[:2], from_y)
    from_y = swap(upper[1], along_y)
    from_x = swap(lower[1], along_x)
    return add(upper[0], from_y), add(lower[0], from_x)


def gather_first(upper, lower, sub):
    along_x, core, along_y = 1, sub, 2 * sub
    lower_x = swap(lower, along_x)
    upper_y = swap(upper, along_y)
    lower_core = swap(lower, core)
    late, lower_core = lax.optimization_barrier(((upper, lower), lower_core))
    upper_x = swap(late[0], along_x)
    lower_y = swap(late[1], along_y)
    upper_xy = swap(upper_y, along_x)
    lower_xy = swap(lower_x, along_y)
    strips = [upper, lower, swap(upper, core), lower_core, upper_x, lower_x, upper_y, lower_y]
    full = spread_halves(strips, [0, core, along_x, along_y])
    rest = [swap(value, core) for value in strips[4:]]
    far, full = lax.optimization_barrier(((upper_xy, lower_xy), full))
    return full, [*rest, *far, *[swap(value, core) for value in far]]


def gather_second(upper, lower, strip, sub, first_work, second_work):
    along_x, core, along_y = 1, sub, 2 * sub
    dtype = strip.dtype
    lower_x = swap(lower, along_x)
    upper_y = swap(upper, along_y)
    upper_x = swap(upper, along_x)
    lower_y = swap(lower, along_y)
    other = swap(strip, core)
    result = first_work()
    lower_x, upper_y, result = lax.optimization_barrier((lower_x, upper_y, result))
    far = swap(upper_y, along_x), swap(lower_x, along_y)
    result = second_work(result)
    x = jnp.concatenate([upper_x, lower_x])
    y = jnp.concatenate([upper_y, lower_y])
    parts = [strip, other, x, y, swap(x, core), swap(y, core)]
    places = [0, core, along_x, along_y, core + along_x, core + along_y]
    far, result = lax.optimization_barrier((far, result))
    last = [swap(half, core) for half in far]
    full = spread(parts, places, dtype)
    last, full = lax.optimization_barrier((last, full))
    return full, [*far, *last], result


def block_of(index, width):
    return pl.ds(pl.multiple_of(index * width, width), width)


def fill_strip(full, strip, d, blocks, width):
    half = blocks // 2
    head = head_rows(width)
    tail = head + (half - 1) * width
    middle, quarter = width // 2, width // 4
    column = block_of(d, width)
    lower = pl.ds(pl.multiple_of(d * width + middle, middle), middle)
    full[pl.ds(pl.multiple_of(d * width, width), middle), column] = strip[:middle]
    full[lower, pl.ds(pl.multiple_of(d * width, width), middle)] = strip[:middle, middle:].T
    for i in range(2):
        at = pl.ds(pl.multiple_of(d * width + middle + i * quarter, quarter), quarter)
        full[at, lower] = strip[middle : middle + quarter, i * middle : (i + 1) * middle]
    across = strip[head:tail].T
    for k in range(1, half):
        r = block_of(lax.rem(d + k, blocks), width)
        full[r, column] = strip[head + (k - 1) * width : head + k * width]
        full[column, r] = across[:, (k - 1) * width : k * width]
    low = d < half
    c = block_of(jnp.where(low, d, d - half), width)
    start = jnp.where(low, (d + half) * width, d * width + middle)
    r = pl.ds(pl.multiple_of(start, middle), middle)
    piece = strip[tail:]
    full[r, c] = piece
    full[c, r] = piece.T


def spread_kernel(places, *refs):
    full = refs[-1]
    blocks = lax.axis_size(team)
    width = full.shape[0] // blocks
    for i, mask in enumerate(places):
        fill_strip(full, refs[i], member_index() ^ mask, blocks, width)


def spread(strips, places, dtype):
    height, width = strips[0].shape
    rows = width * lax.axis_size(team)
    return pl.pallas_call(
        functools.partial(spread_kernel, places),
        in_specs=[ONCHIP] * len(strips),
        out_specs=ONCHIP,
        out_shape=pltpu.VMEM((rows, rows), dtype),
        compiler_params=params(16),
        cost_estimate=pl.CostEstimate(
            flops=height * width * 256 * len(strips),
            bytes_accessed=6 * len(strips) * height * width,
            transcendentals=0,
        ),
        name="spread",
    )(*[in_vmem(strip) for strip in strips])


def fill_halves(full, halves, places, strip):
    blocks = lax.axis_size(team)
    width = full.shape[0] // blocks
    cut = strip.shape[0] // 2
    for i, mask in enumerate(places):
        strip[:cut] = halves[2 * i][...]
        strip[cut:] = halves[2 * i + 1][...]
        fill_strip(full, strip, member_index() ^ mask, blocks, width)


def spread_halves_kernel(places, *refs):
    full, strip = refs[-2:]
    fill_halves(full, refs[:-2], places, strip)


def spread_halves(halves, places):
    cut, width = halves[0].shape
    rows = width * lax.axis_size(team)
    return pl.pallas_call(
        functools.partial(spread_halves_kernel, places),
        in_specs=[ONCHIP] * len(halves),
        out_specs=ONCHIP,
        out_shape=pltpu.VMEM((rows, rows), halves[0].dtype),
        scratch_shapes=[pltpu.VMEM((2 * cut, width), halves[0].dtype)],
        compiler_params=params(16),
        cost_estimate=pl.CostEstimate(
            flops=2 * cut * width * 256 * len(places),
            bytes_accessed=12 * cut * width * len(places),
            transcendentals=0,
        ),
        name="spread_halves",
    )(*[in_vmem(half) for half in halves])


def polynomial_kernel(chunk, *refs):
    halves = refs[1:-6]
    full, upper_out, lower_out, out, poly, middle = refs[-6:]
    rows = full.shape[0]
    packed, width = out.shape
    blocks = rows // width
    half = blocks // 2
    _, _, _, both, _, far_x, far_y, far_both = masks(lax.axis_size("sub"))
    fill_halves(full, halves, [far_x, far_y, both, far_both], out)
    index = member_index()
    mine = block_of(index, width)

    @pl.loop(0, rows // chunk)
    def _(r):
        at = block_of(r, chunk)
        value = cubic_weight * full[at, mine].astype(jnp.float32) + quintic_weight * dot(
            full[at, :], full[:, mine]
        )
        row = lax.broadcasted_iota(jnp.int32, value.shape, 0) + r * chunk
        col = lax.broadcasted_iota(jnp.int32, value.shape, 1) + index * width
        value = value + jnp.where(row == col, linear_weight, 0.0)
        poly[at, :] = value.astype(poly.dtype)

    @pl.loop(0, rows // chunk)
    def _(r):
        at = block_of(r, chunk)
        middle[at, :] = dot(full[at, :], poly[...]).astype(middle.dtype)

    @pl.loop(0, rows // chunk)
    def _(r):
        at = block_of(r, chunk)
        poly[at, :] = (
            cubic_weight * middle[at, :].astype(jnp.float32)
            + quintic_weight * dot(full[at, :], middle[...])
        ).astype(poly.dtype)

    def last(at, cols):
        value = linear_weight * middle[at, cols].astype(jnp.float32)
        return (value + dot(full[at, :], poly[:, cols])).astype(out.dtype)

    every_col = slice(0, width)
    head = head_rows(width)
    tail = head + (half - 1) * width
    write_head(out, last(mine, every_col))
    for k in range(1, half):
        at = block_of(lax.rem(index + k, blocks), width)
        out[head + (k - 1) * width : head + k * width] = last(at, every_col)
    other = pl.multiple_of(lax.rem(index + half, blocks) * width, width)

    @pl.when(index < half)
    def _():
        out[tail:] = last(pl.ds(other, width // 2), every_col)

    @pl.when(index >= half)
    def _():
        out[tail:] = last(pl.ds(other, width), slice(width // 2, width)).T

    upper_out[...] = out[: packed // 2]
    lower_out[...] = out[packed // 2 :]


def polynomial(full, halves):
    cut, width = halves[0].shape
    rows = full.shape[0]
    dtype = full.dtype
    return pl.pallas_call(
        functools.partial(polynomial_kernel, 1024),
        in_specs=[ONCHIP] * (1 + len(halves)),
        input_output_aliases={0: 0},
        out_specs=[ONCHIP] * 4,
        out_shape=[
            pltpu.VMEM((rows, rows), dtype),
            pltpu.VMEM((cut, width), dtype),
            pltpu.VMEM((cut, width), dtype),
            pltpu.VMEM((2 * cut, width), dtype),
        ],
        scratch_shapes=[pltpu.VMEM((rows, width), dtype)] * 2,
        compiler_params=params(16),
        cost_estimate=pl.CostEstimate(
            flops=8 * rows * rows * width, bytes_accessed=4 * rows * rows, transcendentals=0
        ),
        name="polynomial",
    )(in_vmem(full), *[in_vmem(half) for half in halves])


def columns(cols, first=0):
    return [slice(c, min(c + 256, cols)) for c in range(first, cols, 256)]


LATE = 256


def product_kernel(
    chunk, gram_ref, x_ref, o_ref, gram_out, late_out, late_product_out, late_product, sems
):
    rows, cols = o_ref.shape
    stores = [
        pltpu.make_async_copy(gram_ref, gram_out, sems.at[0]),
        pltpu.make_async_copy(x_ref.at[:, cols:], late_out, sems.at[1]),
    ]
    for store in stores:
        store.start()

    @pl.loop(0, rows // chunk)
    def _(r):
        at = block_of(r, chunk)
        late_product[at, :] = dot(gram_ref[at, :], x_ref[:, cols:]).astype(o_ref.dtype)

    stores.append(pltpu.make_async_copy(late_product, late_product_out, sems.at[2]))
    stores[2].start()

    @pl.loop(0, rows // chunk)
    def _(r):
        at = block_of(r, chunk)
        for c in columns(cols):
            o_ref[at, c] = dot(gram_ref[at, :], x_ref[:, c]).astype(o_ref.dtype)

    for store in stores:
        store.wait()


def step_start(gram_whole, current):
    rows, cols = current.shape
    dtype = current.dtype
    return pl.pallas_call(
        functools.partial(product_kernel, 1024),
        in_specs=[ONCHIP] * 2,
        out_specs=[ONCHIP, HBM, HBM, HBM],
        out_shape=[
            pltpu.VMEM((rows, cols - LATE), dtype),
            pltpu.HBM((rows, rows), dtype),
            pltpu.HBM((rows, LATE), dtype),
            pltpu.HBM((rows, LATE), dtype),
        ],
        scratch_shapes=[pltpu.VMEM((rows, LATE), dtype), pltpu.SemaphoreType.DMA((3,))],
        compiler_params=params(16),
        cost_estimate=pl.CostEstimate(
            flops=2 * rows * rows * cols, bytes_accessed=4 * rows * rows, transcendentals=0
        ),
        name="product",
    )(in_vmem(gram_whole), in_vmem(current))


def mix_kernel(chunk, gram_ref, x_ref, product_ref, o_ref):
    rows, cols = o_ref.shape

    @pl.loop(0, rows // chunk)
    def _(r):
        at = block_of(r, chunk)
        for c in columns(cols):
            second = dot(gram_ref[at, :], product_ref[:, c])
            o_ref[at, c] = mix(x_ref[at, c], product_ref[at, c], second)


def step_end(gram_whole, current, product):
    rows, cols = product.shape
    return pl.pallas_call(
        functools.partial(mix_kernel, 1024),
        in_specs=[ONCHIP] * 3,
        out_specs=ONCHIP,
        out_shape=pltpu.VMEM((rows, cols), current.dtype),
        compiler_params=params(16),
        cost_estimate=pl.CostEstimate(
            flops=2 * rows * rows * cols, bytes_accessed=2 * rows * rows, transcendentals=0
        ),
        name="mix",
    )(in_vmem(gram_whole), in_vmem(current), in_vmem(product))


SUM_ROWS = 16


def write_pieces(o_ref, value, r, chunk, local_rows, tile):
    cols = value.shape[1]
    per = chunk // local_rows
    for p in range(per):
        for t in range(cols // 128):
            o_ref[r * per + p, (tile + t) * local_rows : (tile + t + 1) * local_rows, :] = value[
                p * local_rows : (p + 1) * local_rows, t * 128 : (t + 1) * 128
            ]


def mix(current, product, second):
    return (
        linear_weight * current.astype(jnp.float32)
        + cubic_weight * product.astype(jnp.float32)
        + quintic_weight * second
    ).astype(current.dtype)


def first_part_kernel(local_rows, chunk, *refs):
    halves, x_ref = refs[:4], refs[5]
    full, gram_out, rest_out, o_ref, sum_ref, strip, product, pieces, sems = refs[6:]
    rows, cols = product.shape
    store_rest = pltpu.make_async_copy(x_ref.at[:, cols:], rest_out, sems.at[0])
    store_rest.start()
    fill_halves(full, halves, masks(lax.axis_size("sub"))[3::4], strip)
    store_gram = pltpu.make_async_copy(full, gram_out, sems.at[1])
    store_gram.start()
    sum_ref[...] = jnp.zeros_like(sum_ref)

    def stores(r):
        at = block_of(r, chunk // local_rows)
        return pltpu.make_async_copy(pieces.at[at], o_ref.at[at], sems.at[2 + r])

    @pl.loop(0, rows // chunk)
    def _(r):
        at = block_of(r, chunk)
        product[at, :] = dot(full[at, :], x_ref[:, :cols]).astype(product.dtype)

    @pl.loop(0, rows // chunk)
    def _(r):
        at = block_of(r, chunk)
        mixed = mix(x_ref[at, :cols], product[at, :], dot(full[at, :], product[...]))
        write_pieces(pieces, mixed, r, chunk, local_rows, 0)
        stores(r).start()
        value = mixed.astype(jnp.float32)
        sum_ref[...] += jnp.sum(value * value, axis=0, keepdims=True)

    store_rest.wait()
    store_gram.wait()
    for r in range(rows // chunk):
        stores(r).wait()


def first_part(full, halves, current, cols, local_rows):
    cut, width = halves[0].shape
    rows, col_count = current.shape
    dtype = current.dtype
    shape = (rows // local_rows, cols // 128 * local_rows, 128)
    return pl.pallas_call(
        functools.partial(first_part_kernel, local_rows, 1024),
        in_specs=[ONCHIP] * 6,
        out_specs=[ONCHIP, HBM, HBM, HBM, ONCHIP],
        out_shape=[
            pltpu.VMEM((rows, rows), dtype),
            pltpu.HBM((rows, rows), dtype),
            pltpu.HBM((rows, col_count - cols), dtype),
            pltpu.HBM(shape, dtype),
            pltpu.VMEM((1, cols), jnp.float32),
        ],
        input_output_aliases={4: 0},
        scratch_shapes=[
            pltpu.VMEM((2 * cut, width), dtype),
            pltpu.VMEM((rows, cols), dtype),
            pltpu.VMEM(shape, dtype),
            pltpu.SemaphoreType.DMA((2 + rows // 1024,)),
        ],
        compiler_params=params(16),
        cost_estimate=pl.CostEstimate(
            flops=4 * rows * rows * cols, bytes_accessed=4 * rows * rows, transcendentals=0
        ),
        name="first_part",
    )(*[in_vmem(half) for half in halves], in_vmem(full), in_vmem(current))[1:]


def sum_rows(total, dtype):
    high = total.astype(dtype)
    rest = jnp.where(total < jnp.inf, total - high.astype(jnp.float32), 0.0)
    middle = rest.astype(dtype)
    low = rest - middle.astype(jnp.float32)
    row = lax.broadcasted_iota(jnp.int32, (SUM_ROWS, 128), 0)
    parts = jnp.where(row == 0, high.astype(jnp.float32), 0.0)
    parts = jnp.where(row == 1, middle.astype(jnp.float32), parts)
    return jnp.where(row == 2, low, parts).astype(dtype)


def second_part_kernel(
    local_rows,
    chunk,
    before_hbm,
    late_hbm,
    late_product_hbm,
    gram_hbm,
    x_hbm,
    sum_ref,
    o_ref,
    before,
    full,
    late,
    late_product,
    x,
    product,
    total,
    pieces,
    sems,
    block_sems,
):
    rows, cols = x.shape
    count = rows // chunk
    early = cols - late.shape[1]
    body = cols // 128 * local_rows
    load_late = pltpu.make_async_copy(late_hbm, late, sems.at[0])
    load_product = pltpu.make_async_copy(late_product_hbm, late_product, sems.at[1])
    load_x = pltpu.make_async_copy(x_hbm, x.at[:, :early], sems.at[2])

    def loads(k, r):
        source, target = ((before_hbm, before), (gram_hbm, full))[k]
        at = block_of(r, chunk)
        return pltpu.make_async_copy(source.at[at, :], target.at[at, :], block_sems.at[k, r])

    def stores(r):
        at = block_of(r, chunk // local_rows)
        return pltpu.make_async_copy(
            pieces.at[at, :body, :], o_ref.at[at, :body, :], block_sems.at[2, r]
        )

    load_product.start()
    loads(0, 0).start()
    load_late.start()
    load_product.wait()
    load_late.wait()
    load_x.start()

    @pl.loop(0, count)
    def _(r):
        loads(0, r).wait()

        @pl.when(r + 1 < count)
        def _():
            loads(0, r + 1).start()

        @pl.when(r + 1 == count)
        def _():
            loads(1, 0).start()

        at = block_of(r, chunk)
        second = dot(before[at, :], late_product[...])
        x[at, early:] = mix(late[at, :], late_product[at, :], second)

    load_x.wait()

    @pl.loop(0, count)
    def _(r):
        loads(1, r).wait()

        @pl.when(r + 1 < count)
        def _():
            loads(1, r + 1).start()

        at = block_of(r, chunk)
        for c in columns(cols):
            product[at, c] = dot(full[at, :], x[:, c]).astype(product.dtype)

    total[...] = jnp.zeros_like(total)

    @pl.loop(0, count)
    def _(r):
        at = block_of(r, chunk)
        for c in columns(cols):
            mixed = mix(x[at, c], product[at, c], dot(full[at, :], product[:, c]))
            write_pieces(pieces, mixed, r, chunk, local_rows, c.start // 128)
            value = mixed.astype(jnp.float32)
            total[:, c] += jnp.sum(value * value, axis=0, keepdims=True)
        stores(r).start()

    tail = sum_rows(
        jnp.sum(total[...], axis=1, keepdims=True)
        + jnp.sum(sum_ref[...], axis=1, keepdims=True),
        o_ref.dtype,
    )
    for p in range(o_ref.shape[0]):
        pieces[p, body:, :] = tail
    store = pltpu.make_async_copy(pieces.at[:, body:, :], o_ref.at[:, body:, :], sems.at[3])
    store.start()
    for r in range(count):
        stores(r).wait()
    store.wait()


def second_part(before, late, late_product, gram_whole, current, sums, local_rows):
    rows, early = current.shape
    cols = early + late.shape[1]
    dtype = current.dtype
    chunk = 512
    shape = (rows // local_rows, cols // 128 * local_rows + SUM_ROWS, 128)
    return pl.pallas_call(
        functools.partial(second_part_kernel, local_rows, chunk),
        in_specs=[HBM] * 5 + [ONCHIP],
        out_specs=HBM,
        out_shape=pltpu.HBM(shape, dtype),
        scratch_shapes=[
            pltpu.VMEM((rows, rows), dtype),
            pltpu.VMEM((rows, rows), dtype),
            pltpu.VMEM(late.shape, dtype),
            pltpu.VMEM(late.shape, dtype),
            pltpu.VMEM((rows, cols), dtype),
            pltpu.VMEM((rows, cols), dtype),
            pltpu.VMEM((1, cols), jnp.float32),
            pltpu.VMEM(shape, dtype),
            pltpu.SemaphoreType.DMA((4,)),
            pltpu.SemaphoreType.DMA((3, rows // chunk)),
        ],
        compiler_params=params(40),
        cost_estimate=pl.CostEstimate(
            flops=4 * rows * rows * (cols + late.shape[1]),
            bytes_accessed=8 * rows * rows,
            transcendentals=0,
        ),
        name="second_part",
    )(
        *[in_hbm(value) for value in (before, late, late_product, gram_whole, current)],
        in_vmem(sums),
    )


def scaled_kernel(target, first_ref, second_ref, o_ref):
    outer, _, sub, _, _ = first_ref.shape
    local_rows = o_ref.shape[1]
    tiles = first_ref.shape[3] // local_rows
    more = second_ref.shape[3] // local_rows
    total = jnp.zeros((1, 128), jnp.float32)
    for g in range(outer):
        for s in range(sub):
            parts = second_ref[g, 0, s, more * local_rows :, :].astype(jnp.float32)
            total = total + jnp.sum(parts, axis=0, keepdims=True)
    scale = target / (jnp.sqrt(total) + epsilon)
    at = 0
    for g in range(outer):
        for s in range(sub):
            for t in range(tiles + more):
                if t < tiles:
                    value = first_ref[g, 0, s, t * local_rows : (t + 1) * local_rows, :]
                else:
                    u = t - tiles
                    value = second_ref[g, 0, s, u * local_rows : (u + 1) * local_rows, :]
                o_ref[0, :, at : at + 128] = (value.astype(jnp.float32) * scale).astype(
                    o_ref.dtype
                )
                at += 128


def scaled(first, second, local_rows, target):
    outer, mats, sub, height, _ = first.shape
    height_more = second.shape[3]
    cols = outer * sub * 128 * (height // local_rows + height_more // local_rows)
    return pl.pallas_call(
        functools.partial(scaled_kernel, target),
        grid=(mats,),
        in_specs=[
            pl.BlockSpec((outer, 1, sub, height, 128), lambda m: (0, m, 0, 0, 0)),
            pl.BlockSpec((outer, 1, sub, height_more, 128), lambda m: (0, m, 0, 0, 0)),
        ],
        out_specs=pl.BlockSpec((1, local_rows, cols), lambda m: (m, 0, 0)),
        out_shape=jax.ShapeDtypeStruct((mats, local_rows, cols), first.dtype),
        compiler_params=params(14),
        cost_estimate=pl.CostEstimate(
            flops=first.size + second.size,
            bytes_accessed=4 * (first.size + second.size),
            transcendentals=0,
        ),
        name="scaled",
    )(first, second)


def plain_strip(gram, index, width):
    strip = lax.dynamic_slice_in_dim(gram, index * width, width, axis=1)
    row = lax.broadcasted_iota(jnp.int32, strip.shape, 0)
    col = lax.broadcasted_iota(jnp.int32, strip.shape, 1) + index * width
    poly = (
        jnp.where(row == col, linear_weight, 0.0)
        + cubic_weight * strip.astype(jnp.float32)
        + quintic_weight * dot(gram, strip)
    ).astype(jnp.bfloat16)
    middle = dot(gram, poly).astype(jnp.bfloat16)
    middle_f = middle.astype(jnp.float32)
    inner = (cubic_weight * middle_f + quintic_weight * dot(gram, middle)).astype(jnp.bfloat16)
    return (linear_weight * middle_f + dot(gram, inner)).astype(jnp.bfloat16)


def plain_step(gram, current):
    product = dot(gram, current).astype(jnp.bfloat16)
    return mix(current, product, dot(gram, product))


def exchange(pieces):
    return lax.all_to_all(pieces, every, split_axis=0, concat_axis=0, tiled=True)


def kernel_path(iterate, slot_of, outer, groups, sub):
    members = outer * sub
    mats, local_rows, col_count = iterate.shape
    col_width = col_count // members
    rows = local_rows * groups * members
    pieces = pack(iterate, slot_of, outer, sub)
    arrived = exchange(pieces.reshape(mats * members, local_rows, col_width))
    current = arrived.reshape(rows, col_width)
    gram_whole, upper, lower, strip = polynomial(*gather_first(*scatter_sum(current, sub), sub))

    def first_work():
        return step_start(gram_whole, current)

    def second_work(done):
        product, *kept = done
        return step_end(gram_whole, current, product), kept

    full, halves, (stepped, kept) = gather_second(
        upper, lower, strip, sub, first_work, second_work
    )
    whole, rest, first, sums = first_part(full, halves, stepped, 256, local_rows)
    first = exchange(first)
    second = exchange(second_part(*kept, whole, rest, sums, local_rows))
    return scaled(
        first.reshape(outer, mats, sub, -1, 128),
        second.reshape(outer, mats, sub, -1, 128),
        local_rows,
        math.sqrt(rows * col_count),
    )


def plain_path(iterate, slot_of, outer, groups, sub):
    members = outer * sub
    mats, local_rows, col_count = iterate.shape
    col_width = col_count // members
    rows = local_rows * groups * members
    pieces = jnp.take(iterate, slot_of, axis=0)
    pieces = pieces.reshape(mats, local_rows, outer, sub, col_width).transpose(2, 0, 3, 1, 4)
    arrived = exchange(pieces.reshape(mats * members, local_rows, col_width))
    current = arrived.reshape(rows, col_width)
    partial = dot_t(current, current).astype(jnp.bfloat16)
    owned = lax.psum_scatter(partial, team, scatter_dimension=0, tiled=True)
    gram = lax.all_gather(owned, team, axis=0, tiled=True)
    strip = plain_strip(gram, lax.axis_index(team), rows // members)
    gram_next = lax.all_gather(strip.T, team, axis=0, tiled=True)
    current = plain_step(gram, current)
    current = plain_step(gram_next, current)
    values = current.astype(jnp.float32)
    sum_total = lax.psum(jnp.sum(values * values), team)
    scale = math.sqrt(rows * col_count) / (jnp.sqrt(sum_total) + epsilon)
    leaving = (values * scale).astype(jnp.bfloat16)
    returned = exchange(leaving.reshape(groups * members, local_rows, col_width))
    returned = returned.reshape(outer, mats, sub, local_rows, col_width)
    return returned.transpose(1, 3, 0, 2, 4).reshape(mats, local_rows, col_count)


def on_device(iterate, slot_of):
    groups = lax.axis_size("plane")
    sub = lax.axis_size("sub")
    outer = lax.axis_size("grp")
    members = outer * sub
    _, local_rows, col_count = iterate.shape
    col_width = col_count // members
    strip_width = local_rows * groups
    fits = (
        col_width % 128 == 0
        and col_width > 256 + LATE
        and strip_width % 256 == 0
        and local_rows % 16 == 0
        and sub == 2
        and outer == 4
        and groups == 4
    )
    return (kernel_path if fits else plain_path)(iterate, slot_of, outer, groups, sub)


def solution(mesh):
    outer, inner = mesh.devices.shape
    split = Mesh(mesh.devices.reshape(outer, outer, inner // outer), every)
    spec = P(None, every, None)
    return jax.shard_map(
        on_device,
        mesh=split,
        in_specs=(spec, P()),
        out_specs=spec,
        check_vma=False,
    )
```

```python
import functools
import math

import jax
import jax.numpy as jnp
from jax import lax
from jax.experimental import pallas as pl
from jax.experimental.pallas import tpu as pltpu
from jax.sharding import Mesh, PartitionSpec as P

linear_weight = 3.4445
cubic_weight = -4.775
quintic_weight = 2.0315
epsilon = 1e-07

every = ("grp", "plane", "sub")
team = ("grp", "sub")
MIB = 1024 * 1024


def dot(a, b):
    return jnp.dot(a, b, preferred_element_type=jnp.float32)


def dot_t(a, b):
    return lax.dot_general(a, b, (((1,), (1,)), ((), ())), preferred_element_type=jnp.float32)


def params(mib):
    return pltpu.CompilerParams(vmem_limit_bytes=mib * MIB)


def device_index():
    planes = lax.axis_size("plane")
    sub = lax.axis_size("sub")
    return (lax.axis_index("grp") * planes + lax.axis_index("plane")) * sub + lax.axis_index("sub")


def member_index():
    return lax.axis_index("grp") * lax.axis_size("sub") + lax.axis_index("sub")


def in_hbm(value):
    return pltpu.with_memory_space_constraint(value, pltpu.HBM)


def in_vmem(value):
    return pltpu.with_memory_space_constraint(value, pltpu.VMEM)


HBM = pl.BlockSpec(memory_space=pltpu.HBM)
ONCHIP = pl.BlockSpec(memory_space=pltpu.VMEM)


def pack_kernel(slot_ref, x_ref, o_ref, held, load_sems, store_sems):
    outer, mats, sub, _, width = o_ref.shape
    loads = [
        pltpu.make_async_copy(
            x_ref.at[slot_ref[m], rows], held.at[m, rows], load_sems.at[2 * m + i]
        )
        for m in range(mats)
        for i, rows in enumerate((slice(0, held.shape[1] // 2), slice(held.shape[1] // 2, None)))
    ]
    for load in loads:
        load.start()
    stores = []
    for m in range(mats):
        loads[2 * m].wait()
        loads[2 * m + 1].wait()
        for g in range(outer):
            for s in range(sub):
                at = (g * sub + s) * width
                store = pltpu.make_async_copy(
                    held.at[m, :, at : at + width], o_ref.at[g, m, s], store_sems.at[len(stores)]
                )
                store.start()
                stores.append(store)
    for store in stores:
        store.wait()


def pack(iterate, slot_of, outer, sub):
    mats, rows, cols = iterate.shape
    width = cols // (outer * sub)
    return pl.pallas_call(
        pack_kernel,
        grid_spec=pltpu.PrefetchScalarGridSpec(
            num_scalar_prefetch=1,
            grid=(1,),
            in_specs=[HBM],
            out_specs=HBM,
            scratch_shapes=[
                pltpu.VMEM(iterate.shape, iterate.dtype),
                pltpu.SemaphoreType.DMA((2 * mats,)),
                pltpu.SemaphoreType.DMA((mats * outer * sub,)),
            ],
        ),
        out_shape=pltpu.HBM((outer, mats, sub, rows, width), iterate.dtype),
        compiler_params=params(8),
        cost_estimate=pl.CostEstimate(
            flops=0, bytes_accessed=4 * iterate.size, transcendentals=0
        ),
        name="pack",
    )(in_hbm(slot_of), in_hbm(iterate))


def head_rows(width):
    return width // 2 + width // 4


def packed_rows(rows, width):
    return head_rows(width) + (rows // 2 - width) + width // 2


def write_head(o_ref, block):
    half, quarter = block.shape[0] // 2, block.shape[0] // 4
    o_ref[:half] = block[:half]
    o_ref[half : half + quarter, :half] = block[half : half + quarter, half:]
    o_ref[half : half + quarter, half:] = block[half + quarter :, half:]


def gram_strip(x_ref, d, o_ref):
    rows, _ = x_ref.shape
    blocks = lax.axis_size(team)
    width = rows // blocks
    half = blocks // 2
    head = head_rows(width)
    tail = head + (half - 1) * width
    for i in range(blocks):

        @pl.when(d == i)
        def _(i=i):
            mine = x_ref[i * width : (i + 1) * width].T
            first = min(half, blocks - i)
            value = dot(x_ref[i * width : (i + first) * width], mine).astype(o_ref.dtype)
            write_head(o_ref, value[:width])
            split = head + (first - 1) * width
            if first > 1:
                o_ref[head:split] = value[width:]
            if first < half:
                o_ref[split:tail] = dot(x_ref[: (half - first) * width], mine).astype(o_ref.dtype)
            if i < half:
                at = (i + half) * width
                last = dot(x_ref[at : at + width // 2], mine)
            else:
                at = (i - half) * width
                last = dot_t(
                    x_ref[i * width + width // 2 : (i + 1) * width], x_ref[at : at + width]
                )
            o_ref[tail:] = last.astype(o_ref.dtype)


def gram_strips(x_ref, o_ref, masks):
    index = member_index()

    @pl.loop(0, len(masks))
    def _(k):
        mask = masks[0]
        for i, value in enumerate(masks):
            mask = jnp.where(k == i, value, mask)
        gram_strip(x_ref, index ^ mask, o_ref.at[k])


def gram_kernel(masks, x_ref, o_ref):
    gram_strips(x_ref, o_ref, masks)


def gram(current, masks):
    rows, cols = current.shape
    count = len(masks)
    width = rows // lax.axis_size(team)
    packed = packed_rows(rows, width)
    return pl.pallas_call(
        functools.partial(gram_kernel, masks),
        in_specs=[ONCHIP],
        out_specs=ONCHIP,
        out_shape=pltpu.VMEM((count, packed, width), current.dtype),
        compiler_params=params(16),
        cost_estimate=pl.CostEstimate(
            flops=2 * count * packed * width * cols,
            bytes_accessed=2 * (current.size + count * packed * width),
            transcendentals=0,
        ),
        name="gram",
    )(in_vmem(current))


def add(a, b):
    return (a.astype(jnp.float32) + b.astype(jnp.float32)).astype(a.dtype)


def swap(value, mask):
    pairs = [(i, i ^ mask) for i in range(lax.axis_size(team))]
    return lax.ppermute(value, team, pairs)


def masks(sub):
    along_x, core, along_y = 1, sub, 2 * sub
    near = [0, along_x, along_y, along_x + along_y]
    return near + [core + mask for mask in near]


def scatter_sum(current, sub):
    along_x, core, along_y = 1, sub, 2 * sub
    arrived = swap(gram(current, masks(sub)[4:]), core)
    total = add(gram(current, masks(sub)[:4]), arrived)
    cut = total.shape[1] // 2
    upper, lower = total[:, :cut], total[:, cut:]
    from_x = swap(upper[1::2], along_x)
    from_y = swap(lower[2:], along_y)
    upper = add(upper[::2], from_x)
    lower = add(lower[:2], from_y)
    from_y = swap(upper[1], along_y)
    from_x = swap(lower[1], along_x)
    return add(upper[0], from_y), add(lower[0], from_x)


def gather_first(upper, lower, sub):
    along_x, core, along_y = 1, sub, 2 * sub
    lower_x = swap(lower, along_x)
    upper_y = swap(upper, along_y)
    lower_core = swap(lower, core)
    late, lower_core = lax.optimization_barrier(((upper, lower), lower_core))
    upper_x = swap(late[0], along_x)
    lower_y = swap(late[1], along_y)
    upper_xy = swap(upper_y, along_x)
    lower_xy = swap(lower_x, along_y)
    strips = [upper, lower, swap(upper, core), lower_core, upper_x, lower_x, upper_y, lower_y]
    full = spread_halves(strips, [0, core, along_x, along_y])
    rest = [swap(value, core) for value in strips[4:]]
    far, full = lax.optimization_barrier(((upper_xy, lower_xy), full))
    return full, [*rest, *far, *[swap(value, core) for value in far]]


def gather_second(upper, lower, strip, sub, first_work, second_work):
    along_x, core, along_y = 1, sub, 2 * sub
    dtype = strip.dtype
    lower_x = swap(lower, along_x)
    upper_y = swap(upper, along_y)
    upper_x = swap(upper, along_x)
    lower_y = swap(lower, along_y)
    other = swap(strip, core)
    result = first_work()
    lower_x, upper_y, result = lax.optimization_barrier((lower_x, upper_y, result))
    far = swap(upper_y, along_x), swap(lower_x, along_y)
    result = second_work(result)
    x = jnp.concatenate([upper_x, lower_x])
    y = jnp.concatenate([upper_y, lower_y])
    parts = [strip, other, x, y, swap(x, core), swap(y, core)]
    places = [0, core, along_x, along_y, core + along_x, core + along_y]
    far, result = lax.optimization_barrier((far, result))
    last = [swap(half, core) for half in far]
    full = spread(parts, places, dtype)
    last, full = lax.optimization_barrier((last, full))
    return full, [*far, *last], result


def block_of(index, width):
    return pl.ds(pl.multiple_of(index * width, width), width)


def fill_strip(full, strip, d, blocks, width):
    half = blocks // 2
    head = head_rows(width)
    tail = head + (half - 1) * width
    middle, quarter = width // 2, width // 4
    column = block_of(d, width)
    lower = pl.ds(pl.multiple_of(d * width + middle, middle), middle)
    full[pl.ds(pl.multiple_of(d * width, width), middle), column] = strip[:middle]
    full[lower, pl.ds(pl.multiple_of(d * width, width), middle)] = strip[:middle, middle:].T
    for i in range(2):
        at = pl.ds(pl.multiple_of(d * width + middle + i * quarter, quarter), quarter)
        full[at, lower] = strip[middle : middle + quarter, i * middle : (i + 1) * middle]
    across = strip[head:tail].T
    for k in range(1, half):
        r = block_of(lax.rem(d + k, blocks), width)
        full[r, column] = strip[head + (k - 1) * width : head + k * width]
        full[column, r] = across[:, (k - 1) * width : k * width]
    low = d < half
    c = block_of(jnp.where(low, d, d - half), width)
    start = jnp.where(low, (d + half) * width, d * width + middle)
    r = pl.ds(pl.multiple_of(start, middle), middle)
    piece = strip[tail:]
    full[r, c] = piece
    full[c, r] = piece.T


def spread_kernel(places, *refs):
    full = refs[-1]
    blocks = lax.axis_size(team)
    width = full.shape[0] // blocks
    for i, mask in enumerate(places):
        fill_strip(full, refs[i], member_index() ^ mask, blocks, width)


def spread(strips, places, dtype):
    height, width = strips[0].shape
    rows = width * lax.axis_size(team)
    return pl.pallas_call(
        functools.partial(spread_kernel, places),
        in_specs=[ONCHIP] * len(strips),
        out_specs=ONCHIP,
        out_shape=pltpu.VMEM((rows, rows), dtype),
        compiler_params=params(16),
        cost_estimate=pl.CostEstimate(
            flops=height * width * 256 * len(strips),
            bytes_accessed=6 * len(strips) * height * width,
            transcendentals=0,
        ),
        name="spread",
    )(*[in_vmem(strip) for strip in strips])


def fill_halves(full, halves, places, strip):
    blocks = lax.axis_size(team)
    width = full.shape[0] // blocks
    cut = strip.shape[0] // 2
    for i, mask in enumerate(places):
        strip[:cut] = halves[2 * i][...]
        strip[cut:] = halves[2 * i + 1][...]
        fill_strip(full, strip, member_index() ^ mask, blocks, width)


def spread_halves_kernel(places, *refs):
    full, strip = refs[-2:]
    fill_halves(full, refs[:-2], places, strip)


def spread_halves(halves, places):
    cut, width = halves[0].shape
    rows = width * lax.axis_size(team)
    return pl.pallas_call(
        functools.partial(spread_halves_kernel, places),
        in_specs=[ONCHIP] * len(halves),
        out_specs=ONCHIP,
        out_shape=pltpu.VMEM((rows, rows), halves[0].dtype),
        scratch_shapes=[pltpu.VMEM((2 * cut, width), halves[0].dtype)],
        compiler_params=params(16),
        cost_estimate=pl.CostEstimate(
            flops=2 * cut * width * 256 * len(places),
            bytes_accessed=12 * cut * width * len(places),
            transcendentals=0,
        ),
        name="spread_halves",
    )(*[in_vmem(half) for half in halves])


def polynomial_kernel(chunk, *refs):
    halves = refs[1:-6]
    full, upper_out, lower_out, out, poly, middle = refs[-6:]
    rows = full.shape[0]
    packed, width = out.shape
    blocks = rows // width
    half = blocks // 2
    _, _, _, both, _, far_x, far_y, far_both = masks(lax.axis_size("sub"))
    fill_halves(full, halves, [far_x, far_y, both, far_both], out)
    index = member_index()
    mine = block_of(index, width)

    @pl.loop(0, rows // chunk)
    def _(r):
        at = block_of(r, chunk)
        value = cubic_weight * full[at, mine].astype(jnp.float32) + quintic_weight * dot(
            full[at, :], full[:, mine]
        )
        row = lax.broadcasted_iota(jnp.int32, value.shape, 0) + r * chunk
        col = lax.broadcasted_iota(jnp.int32, value.shape, 1) + index * width
        value = value + jnp.where(row == col, linear_weight, 0.0)
        poly[at, :] = value.astype(poly.dtype)

    @pl.loop(0, rows // chunk)
    def _(r):
        at = block_of(r, chunk)
        middle[at, :] = dot(full[at, :], poly[...]).astype(middle.dtype)

    @pl.loop(0, rows // chunk)
    def _(r):
        at = block_of(r, chunk)
        poly[at, :] = (
            cubic_weight * middle[at, :].astype(jnp.float32)
            + quintic_weight * dot(full[at, :], middle[...])
        ).astype(poly.dtype)

    def last(at, cols):
        value = linear_weight * middle[at, cols].astype(jnp.float32)
        return (value + dot(full[at, :], poly[:, cols])).astype(out.dtype)

    every_col = slice(0, width)
    head = head_rows(width)
    tail = head + (half - 1) * width
    write_head(out, last(mine, every_col))
    for k in range(1, half):
        at = block_of(lax.rem(index + k, blocks), width)
        out[head + (k - 1) * width : head + k * width] = last(at, every_col)
    other = pl.multiple_of(lax.rem(index + half, blocks) * width, width)

    @pl.when(index < half)
    def _():
        out[tail:] = last(pl.ds(other, width // 2), every_col)

    @pl.when(index >= half)
    def _():
        out[tail:] = last(pl.ds(other, width), slice(width // 2, width)).T

    upper_out[...] = out[: packed // 2]
    lower_out[...] = out[packed // 2 :]


def polynomial(full, halves):
    cut, width = halves[0].shape
    rows = full.shape[0]
    dtype = full.dtype
    return pl.pallas_call(
        functools.partial(polynomial_kernel, 1024),
        in_specs=[ONCHIP] * (1 + len(halves)),
        input_output_aliases={0: 0},
        out_specs=[ONCHIP] * 4,
        out_shape=[
            pltpu.VMEM((rows, rows), dtype),
            pltpu.VMEM((cut, width), dtype),
            pltpu.VMEM((cut, width), dtype),
            pltpu.VMEM((2 * cut, width), dtype),
        ],
        scratch_shapes=[pltpu.VMEM((rows, width), dtype)] * 2,
        compiler_params=params(16),
        cost_estimate=pl.CostEstimate(
            flops=8 * rows * rows * width, bytes_accessed=4 * rows * rows, transcendentals=0
        ),
        name="polynomial",
    )(in_vmem(full), *[in_vmem(half) for half in halves])


def columns(cols, first=0):
    return [slice(c, min(c + 256, cols)) for c in range(first, cols, 256)]


LATE = 256


def product_kernel(
    chunk, gram_ref, x_ref, o_ref, gram_out, late_out, late_product_out, late_product, sems
):
    rows, cols = o_ref.shape
    stores = [
        pltpu.make_async_copy(gram_ref, gram_out, sems.at[0]),
        pltpu.make_async_copy(x_ref.at[:, cols:], late_out, sems.at[1]),
    ]
    for store in stores:
        store.start()

    @pl.loop(0, rows // chunk)
    def _(r):
        at = block_of(r, chunk)
        late_product[at, :] = dot(gram_ref[at, :], x_ref[:, cols:]).astype(o_ref.dtype)

    stores.append(pltpu.make_async_copy(late_product, late_product_out, sems.at[2]))
    stores[2].start()

    @pl.loop(0, rows // chunk)
    def _(r):
        at = block_of(r, chunk)
        for c in columns(cols):
            o_ref[at, c] = dot(gram_ref[at, :], x_ref[:, c]).astype(o_ref.dtype)

    for store in stores:
        store.wait()


def step_start(gram_whole, current):
    rows, cols = current.shape
    dtype = current.dtype
    return pl.pallas_call(
        functools.partial(product_kernel, 1024),
        in_specs=[ONCHIP] * 2,
        out_specs=[ONCHIP, HBM, HBM, HBM],
        out_shape=[
            pltpu.VMEM((rows, cols - LATE), dtype),
            pltpu.HBM((rows, rows), dtype),
            pltpu.HBM((rows, LATE), dtype),
            pltpu.HBM((rows, LATE), dtype),
        ],
        scratch_shapes=[pltpu.VMEM((rows, LATE), dtype), pltpu.SemaphoreType.DMA((3,))],
        compiler_params=params(16),
        cost_estimate=pl.CostEstimate(
            flops=2 * rows * rows * cols, bytes_accessed=4 * rows * rows, transcendentals=0
        ),
        name="product",
    )(in_vmem(gram_whole), in_vmem(current))


def mix_kernel(chunk, gram_ref, x_ref, product_ref, o_ref):
    rows, cols = o_ref.shape

    @pl.loop(0, rows // chunk)
    def _(r):
        at = block_of(r, chunk)
        for c in columns(cols):
            second = dot(gram_ref[at, :], product_ref[:, c])
            o_ref[at, c] = mix(x_ref[at, c], product_ref[at, c], second)


def step_end(gram_whole, current, product):
    rows, cols = product.shape
    return pl.pallas_call(
        functools.partial(mix_kernel, 1024),
        in_specs=[ONCHIP] * 3,
        out_specs=ONCHIP,
        out_shape=pltpu.VMEM((rows, cols), current.dtype),
        compiler_params=params(16),
        cost_estimate=pl.CostEstimate(
            flops=2 * rows * rows * cols, bytes_accessed=2 * rows * rows, transcendentals=0
        ),
        name="mix",
    )(in_vmem(gram_whole), in_vmem(current), in_vmem(product))


SUM_ROWS = 16


def write_pieces(o_ref, value, r, chunk, local_rows, tile):
    cols = value.shape[1]
    per = chunk // local_rows
    for p in range(per):
        for t in range(cols // 128):
            o_ref[r * per + p, (tile + t) * local_rows : (tile + t + 1) * local_rows, :] = value[
                p * local_rows : (p + 1) * local_rows, t * 128 : (t + 1) * 128
            ]


def mix(current, product, second):
    return (
        linear_weight * current.astype(jnp.float32)
        + cubic_weight * product.astype(jnp.float32)
        + quintic_weight * second
    ).astype(current.dtype)


def first_part_kernel(local_rows, chunk, *refs):
    halves, x_ref = refs[:4], refs[5]
    full, gram_out, rest_out, o_ref, sum_ref, strip, product, pieces, sems = refs[6:]
    rows, cols = product.shape
    store_rest = pltpu.make_async_copy(x_ref.at[:, cols:], rest_out, sems.at[0])
    store_rest.start()
    fill_halves(full, halves, masks(lax.axis_size("sub"))[3::4], strip)
    store_gram = pltpu.make_async_copy(full, gram_out, sems.at[1])
    store_gram.start()
    sum_ref[...] = jnp.zeros_like(sum_ref)

    def stores(r):
        at = block_of(r, chunk // local_rows)
        return pltpu.make_async_copy(pieces.at[at], o_ref.at[at], sems.at[2 + r])

    @pl.loop(0, rows // chunk)
    def _(r):
        at = block_of(r, chunk)
        product[at, :] = dot(full[at, :], x_ref[:, :cols]).astype(product.dtype)

    @pl.loop(0, rows // chunk)
    def _(r):
        at = block_of(r, chunk)
        mixed = mix(x_ref[at, :cols], product[at, :], dot(full[at, :], product[...]))
        write_pieces(pieces, mixed, r, chunk, local_rows, 0)
        stores(r).start()
        value = mixed.astype(jnp.float32)
        sum_ref[...] += jnp.sum(value * value, axis=0, keepdims=True)

    store_rest.wait()
    store_gram.wait()
    for r in range(rows // chunk):
        stores(r).wait()


def first_part(full, halves, current, cols, local_rows):
    cut, width = halves[0].shape
    rows, col_count = current.shape
    dtype = current.dtype
    shape = (rows // local_rows, cols // 128 * local_rows, 128)
    return pl.pallas_call(
        functools.partial(first_part_kernel, local_rows, 1024),
        in_specs=[ONCHIP] * 6,
        out_specs=[ONCHIP, HBM, HBM, HBM, ONCHIP],
        out_shape=[
            pltpu.VMEM((rows, rows), dtype),
            pltpu.HBM((rows, rows), dtype),
            pltpu.HBM((rows, col_count - cols), dtype),
            pltpu.HBM(shape, dtype),
            pltpu.VMEM((1, cols), jnp.float32),
        ],
        input_output_aliases={4: 0},
        scratch_shapes=[
            pltpu.VMEM((2 * cut, width), dtype),
            pltpu.VMEM((rows, cols), dtype),
            pltpu.VMEM(shape, dtype),
            pltpu.SemaphoreType.DMA((2 + rows // 1024,)),
        ],
        compiler_params=params(16),
        cost_estimate=pl.CostEstimate(
            flops=4 * rows * rows * cols, bytes_accessed=4 * rows * rows, transcendentals=0
        ),
        name="first_part",
    )(*[in_vmem(half) for half in halves], in_vmem(full), in_vmem(current))[1:]


def sum_rows(total, dtype):
    high = total.astype(dtype)
    rest = jnp.where(total < jnp.inf, total - high.astype(jnp.float32), 0.0)
    middle = rest.astype(dtype)
    low = rest - middle.astype(jnp.float32)
    row = lax.broadcasted_iota(jnp.int32, (SUM_ROWS, 128), 0)
    parts = jnp.where(row == 0, high.astype(jnp.float32), 0.0)
    parts = jnp.where(row == 1, middle.astype(jnp.float32), parts)
    return jnp.where(row == 2, low, parts).astype(dtype)


def second_part_kernel(
    local_rows,
    chunk,
    before_hbm,
    late_hbm,
    late_product_hbm,
    gram_hbm,
    x_hbm,
    sum_ref,
    o_ref,
    before,
    full,
    late,
    late_product,
    x,
    product,
    total,
    pieces,
    sems,
    block_sems,
):
    rows, cols = x.shape
    count = rows // chunk
    early = cols - late.shape[1]
    body = cols // 128 * local_rows
    load_late = pltpu.make_async_copy(late_hbm, late, sems.at[0])
    load_product = pltpu.make_async_copy(late_product_hbm, late_product, sems.at[1])
    load_x = pltpu.make_async_copy(x_hbm, x.at[:, :early], sems.at[2])

    def loads(k, r):
        source, target = ((before_hbm, before), (gram_hbm, full))[k]
        at = block_of(r, chunk)
        return pltpu.make_async_copy(source.at[at, :], target.at[at, :], block_sems.at[k, r])

    def stores(r):
        at = block_of(r, chunk // local_rows)
        return pltpu.make_async_copy(
            pieces.at[at, :body, :], o_ref.at[at, :body, :], block_sems.at[2, r]
        )

    load_product.start()
    loads(0, 0).start()
    load_late.start()
    load_product.wait()
    load_late.wait()
    load_x.start()

    @pl.loop(0, count)
    def _(r):
        loads(0, r).wait()

        @pl.when(r + 1 < count)
        def _():
            loads(0, r + 1).start()

        @pl.when(r + 1 == count)
        def _():
            loads(1, 0).start()

        at = block_of(r, chunk)
        second = dot(before[at, :], late_product[...])
        x[at, early:] = mix(late[at, :], late_product[at, :], second)

    load_x.wait()

    @pl.loop(0, count)
    def _(r):
        loads(1, r).wait()

        @pl.when(r + 1 < count)
        def _():
            loads(1, r + 1).start()

        at = block_of(r, chunk)
        for c in columns(cols):
            product[at, c] = dot(full[at, :], x[:, c]).astype(product.dtype)

    total[...] = jnp.zeros_like(total)

    @pl.loop(0, count)
    def _(r):
        at = block_of(r, chunk)
        for c in columns(cols):
            mixed = mix(x[at, c], product[at, c], dot(full[at, :], product[:, c]))
            write_pieces(pieces, mixed, r, chunk, local_rows, c.start // 128)
            value = mixed.astype(jnp.float32)
            total[:, c] += jnp.sum(value * value, axis=0, keepdims=True)
        stores(r).start()

    tail = sum_rows(
        jnp.sum(total[...], axis=1, keepdims=True)
        + jnp.sum(sum_ref[...], axis=1, keepdims=True),
        o_ref.dtype,
    )
    for p in range(o_ref.shape[0]):
        pieces[p, body:, :] = tail
    store = pltpu.make_async_copy(pieces.at[:, body:, :], o_ref.at[:, body:, :], sems.at[3])
    store.start()
    for r in range(count):
        stores(r).wait()
    store.wait()


def second_part(before, late, late_product, gram_whole, current, sums, local_rows):
    rows, early = current.shape
    cols = early + late.shape[1]
    dtype = current.dtype
    chunk = 512
    shape = (rows // local_rows, cols // 128 * local_rows + SUM_ROWS, 128)
    return pl.pallas_call(
        functools.partial(second_part_kernel, local_rows, chunk),
        in_specs=[HBM] * 5 + [ONCHIP],
        out_specs=HBM,
        out_shape=pltpu.HBM(shape, dtype),
        scratch_shapes=[
            pltpu.VMEM((rows, rows), dtype),
            pltpu.VMEM((rows, rows), dtype),
            pltpu.VMEM(late.shape, dtype),
            pltpu.VMEM(late.shape, dtype),
            pltpu.VMEM((rows, cols), dtype),
            pltpu.VMEM((rows, cols), dtype),
            pltpu.VMEM((1, cols), jnp.float32),
            pltpu.VMEM(shape, dtype),
            pltpu.SemaphoreType.DMA((4,)),
            pltpu.SemaphoreType.DMA((3, rows // chunk)),
        ],
        compiler_params=params(40),
        cost_estimate=pl.CostEstimate(
            flops=4 * rows * rows * (cols + late.shape[1]),
            bytes_accessed=8 * rows * rows,
            transcendentals=0,
        ),
        name="second_part",
    )(
        *[in_hbm(value) for value in (before, late, late_product, gram_whole, current)],
        in_vmem(sums),
    )


def scaled_kernel(target, first_ref, second_ref, o_ref):
    outer, _, sub, _, _ = first_ref.shape
    local_rows = o_ref.shape[1]
    tiles = first_ref.shape[3] // local_rows
    more = second_ref.shape[3] // local_rows
    total = jnp.zeros((1, 128), jnp.float32)
    for g in range(outer):
        for s in range(sub):
            parts = second_ref[g, 0, s, more * local_rows :, :].astype(jnp.float32)
            total = total + jnp.sum(parts, axis=0, keepdims=True)
    scale = target / (jnp.sqrt(total) + epsilon)
    at = 0
    for g in range(outer):
        for s in range(sub):
            for t in range(tiles + more):
                if t < tiles:
                    value = first_ref[g, 0, s, t * local_rows : (t + 1) * local_rows, :]
                else:
                    u = t - tiles
                    value = second_ref[g, 0, s, u * local_rows : (u + 1) * local_rows, :]
                o_ref[0, :, at : at + 128] = (value.astype(jnp.float32) * scale).astype(
                    o_ref.dtype
                )
                at += 128


def scaled(first, second, local_rows, target):
    outer, mats, sub, height, _ = first.shape
    height_more = second.shape[3]
    cols = outer * sub * 128 * (height // local_rows + height_more // local_rows)
    return pl.pallas_call(
        functools.partial(scaled_kernel, target),
        grid=(mats,),
        in_specs=[
            pl.BlockSpec((outer, 1, sub, height, 128), lambda m: (0, m, 0, 0, 0)),
            pl.BlockSpec((outer, 1, sub, height_more, 128), lambda m: (0, m, 0, 0, 0)),
        ],
        out_specs=pl.BlockSpec((1, local_rows, cols), lambda m: (m, 0, 0)),
        out_shape=jax.ShapeDtypeStruct((mats, local_rows, cols), first.dtype),
        compiler_params=params(14),
        cost_estimate=pl.CostEstimate(
            flops=first.size + second.size,
            bytes_accessed=4 * (first.size + second.size),
            transcendentals=0,
        ),
        name="scaled",
    )(first, second)


def plain_strip(gram, index, width):
    strip = lax.dynamic_slice_in_dim(gram, index * width, width, axis=1)
    row = lax.broadcasted_iota(jnp.int32, strip.shape, 0)
    col = lax.broadcasted_iota(jnp.int32, strip.shape, 1) + index * width
    poly = (
        jnp.where(row == col, linear_weight, 0.0)
        + cubic_weight * strip.astype(jnp.float32)
        + quintic_weight * dot(gram, strip)
    ).astype(jnp.bfloat16)
    middle = dot(gram, poly).astype(jnp.bfloat16)
    middle_f = middle.astype(jnp.float32)
    inner = (cubic_weight * middle_f + quintic_weight * dot(gram, middle)).astype(jnp.bfloat16)
    return (linear_weight * middle_f + dot(gram, inner)).astype(jnp.bfloat16)


def plain_step(gram, current):
    product = dot(gram, current).astype(jnp.bfloat16)
    return mix(current, product, dot(gram, product))


def exchange(pieces):
    return lax.all_to_all(pieces, every, split_axis=0, concat_axis=0, tiled=True)


def kernel_path(iterate, slot_of, outer, groups, sub):
    members = outer * sub
    mats, local_rows, col_count = iterate.shape
    col_width = col_count // members
    rows = local_rows * groups * members
    pieces = pack(iterate, slot_of, outer, sub)
    arrived = exchange(pieces.reshape(mats * members, local_rows, col_width))
    current = arrived.reshape(rows, col_width)
    gram_whole, upper, lower, strip = polynomial(*gather_first(*scatter_sum(current, sub), sub))

    def first_work():
        return step_start(gram_whole, current)

    def second_work(done):
        product, *kept = done
        return step_end(gram_whole, current, product), kept

    full, halves, (stepped, kept) = gather_second(
        upper, lower, strip, sub, first_work, second_work
    )
    whole, rest, first, sums = first_part(full, halves, stepped, 256, local_rows)
    first = exchange(first)
    second = exchange(second_part(*kept, whole, rest, sums, local_rows))
    return scaled(
        first.reshape(outer, mats, sub, -1, 128),
        second.reshape(outer, mats, sub, -1, 128),
        local_rows,
        math.sqrt(rows * col_count),
    )


def plain_path(iterate, slot_of, outer, groups, sub):
    members = outer * sub
    mats, local_rows, col_count = iterate.shape
    col_width = col_count // members
    rows = local_rows * groups * members
    pieces = jnp.take(iterate, slot_of, axis=0)
    pieces = pieces.reshape(mats, local_rows, outer, sub, col_width).transpose(2, 0, 3, 1, 4)
    arrived = exchange(pieces.reshape(mats * members, local_rows, col_width))
    current = arrived.reshape(rows, col_width)
    partial = dot_t(current, current).astype(jnp.bfloat16)
    owned = lax.psum_scatter(partial, team, scatter_dimension=0, tiled=True)
    gram = lax.all_gather(owned, team, axis=0, tiled=True)
    strip = plain_strip(gram, lax.axis_index(team), rows // members)
    gram_next = lax.all_gather(strip.T, team, axis=0, tiled=True)
    current = plain_step(gram, current)
    current = plain_step(gram_next, current)
    values = current.astype(jnp.float32)
    sum_total = lax.psum(jnp.sum(values * values), team)
    scale = math.sqrt(rows * col_count) / (jnp.sqrt(sum_total) + epsilon)
    leaving = (values * scale).astype(jnp.bfloat16)
    returned = exchange(leaving.reshape(groups * members, local_rows, col_width))
    returned = returned.reshape(outer, mats, sub, local_rows, col_width)
    return returned.transpose(1, 3, 0, 2, 4).reshape(mats, local_rows, col_count)


def on_device(iterate, slot_of):
    groups = lax.axis_size("plane")
    sub = lax.axis_size("sub")
    outer = lax.axis_size("grp")
    members = outer * sub
    _, local_rows, col_count = iterate.shape
    col_width = col_count // members
    strip_width = local_rows * groups
    fits = (
        col_width % 128 == 0
        and col_width > 256 + LATE
        and strip_width % 256 == 0
        and local_rows % 16 == 0
        and sub == 2
        and outer == 4
        and groups == 4
    )
    return (kernel_path if fits else plain_path)(iterate, slot_of, outer, groups, sub)


def solution(mesh):
    outer, inner = mesh.devices.shape
    split = Mesh(mesh.devices.reshape(outer, outer, inner // outer), every)
    spec = P(None, every, None)
    return jax.shard_map(
        on_device,
        mesh=split,
        in_specs=(spec, P()),
        out_specs=spec,
        check_vma=False,
    )
```
